32 devices in a mesh: lat: 4 (over z), lon: 8 (over y, x, core).
Axes of the slice: x: 2, y: 2, z: 4, core: 2. Of those that a mesh axis runs over, the one named last changes fastest.
Arguments:
- corona: float32 [8, 64, 128, 128], P(None, 'lat', 'lon'), may hold values from -6 to 6
- kappa: float32 [64, 128, 128], P('lat', 'lon'), may hold values from 0.05 to 1
- mixing: float32 [8, 8], replicated, may hold values from -2 to 2
- helio_prev: float32 [8, 256, 512], P(None, 'lon', 'lat'), may hold values from -6 to 6
- owner: int32 [65536, 1], P(('lat', 'lon')), may hold values from 0 to 31; in each aligned block of 2048 rows (0 to 2047, 2048 to 4095, ...) at most 128 rows name the same one
- dest_cell: int32 [65536], P(('lat', 'lon')), may hold values from 0 to 4095
- corner_base: int32 [65536], P(('lat', 'lon')), may hold values from 0 to 1910, as said below
- fractions: float32 [3, 65536], P(None, ('lat', 'lon')), may hold values from 0 to 1
Outputs:
- stepped: float32 [8, 64, 128, 128], P(None, 'lat', 'lon')
- helio_face: float32 [8, 256, 512], P(None, 'lon', 'lat')
The draws below stay inside these ranges and needn't reach their ends.
Inputs may be any that keep to these rules, and one draw needn't show every extreme that they name: Among the targets of one device no owner appears more than 128 times, a bound that some block reaches. corner_base = (t * 16 + p) * 8 + r with t < 15, p < 15, r < 7.
All inputs are finite; a program needn't handle non-finite values.
Results may differ from the reference program's by a relative error of at most 0.000075.
Values sent between devices are 32-bit elements; how exact they have to be, the bound alone decides.
A program may use at most 64 MiB of HBM per device.

```python
import math
import jax
import jax.numpy as jnp
import numpy as np
from jax import lax

FIELDS = 8
CT = 16
CP = 16
NR = 128
SH = 8
T_DEV = 2048
FP = 32
FT = 128
NT = 64
NP = 128
NFP = 256
NFT = 512
TARGETS = 65536
CAP = 128
N_LON = 8
DEVICES = 32


def draw_corner_base(key, part):
    key_t, key_p, key_r = jax.random.split(jax.random.fold_in(key, 7), 3)
    theta = jax.random.randint(key_t, (TARGETS,), 0, CT - 1)
    phi = jax.random.randint(key_p, (TARGETS,), 0, CP - 1)
    layer = jax.random.randint(key_r, (TARGETS,), 0, SH - 1)
    return ((theta * CP + phi) * SH + layer).astype(jnp.int32)


def touch_ends(drawn, rng, smallest, largest):
    longest = drawn.shape.index(max(drawn.shape))
    spots = []
    for shift in (0, 1):
        where = [jax.random.randint(jax.random.fold_in(rng, axis), (), 0, length) for axis, length in enumerate(drawn.shape)]
        where[longest] = (where[longest] + shift) % drawn.shape[longest]
        spots.append(tuple(where))
    return drawn.at[spots[0]].set(smallest).at[spots[1]].set(largest)


def block_levels(own_key, extent, cuts, low, top_value):
    def one(dim, parts):
        steps = jax.random.uniform(jax.random.fold_in(jax.random.fold_in(own_key, 6), dim), (parts,), jnp.float32, low / len(cuts), top_value / len(cuts))
        return jnp.repeat(jnp.exp(steps), extent[dim] // parts).reshape((-1,) + (1,) * (len(extent) - dim - 1))

    gain = one(*cuts[0])
    for cut in cuts[1:]:
        gain = gain * one(*cut)
    return gain


def deal_out(own_key, own, number, rows, amount, top, reach, slope):
    order = jax.random.permutation(own_key, amount)
    crowded, common = portions_of(amount, rows * top, reach, slope, True), portions_of(amount, rows * top, reach, slope, False)
    places = jnp.arange(amount)

    def named(lengths, offset_by):
        used = int((lengths > 0).sum())
        fixed = max(1, used // 4)
        passed = fixed + (places - fixed + offset_by * (used - fixed)) % max(1, amount - fixed)
        return jnp.zeros((amount,), jnp.int32).at[order[jnp.where(places < fixed, places, passed)]].set(jnp.asarray(lengths, jnp.int32))

    lengths = jnp.where(number % 4 == 0, named(crowded, number // 4), named(common, number - number // 4 - 1))
    mixed = jax.random.permutation(jax.random.fold_in(own, 3), amount)
    source_of, sink = mixed[0:amount // 2 * 2:2], mixed[1:amount // 2 * 2:2]
    margin = jnp.minimum(lengths[source_of] - 1, reach - lengths[sink]) // 2
    margin = jnp.where((source_of == order[0]) | (sink == order[0]) | (lengths[sink] == 0), 0, jnp.maximum(margin, 0))
    passed = jax.random.randint(jax.random.fold_in(own, 4), (amount // 2,), 0, 1 << 20) % (margin + 1)
    lengths = lengths.at[source_of].add(-passed).at[sink].add(passed)
    members = jnp.searchsorted(jnp.cumsum(lengths), jnp.arange(rows * top), side="right").astype(jnp.int32)
    grid = members.reshape(top, rows).T
    grid = grid[jax.random.permutation(jax.random.fold_in(own, 1), rows)]
    offset_by = jax.random.randint(jax.random.fold_in(own, 2), (rows, 1), 0, top)
    return jnp.take_along_axis(grid, (jnp.arange(top)[None, :] + offset_by) % top, axis=1)


def portions_of(number_of, total, most, lean, full):
    loads = [(1 << 20) // math.isqrt(rank ** lean) + 1 for rank in range(1, number_of + 1)]
    largest = most if full else min(most, max(-(-total // number_of), total * loads[0] // sum(loads)))
    least = 1 if total - largest >= number_of - 1 else 0
    holding, rest = [largest] + [least] * (number_of - 1), total - largest - least * (number_of - 1)
    while rest > 0:
        movable = [i for i in range(1, number_of) if holding[i] < largest] or [i for i in range(1, number_of) if holding[i] < most]
        pool, remaining = sum([loads[i] for i in movable]), rest
        for i in movable:
            more = min(most - holding[i], max(1, remaining * loads[i] // pool), rest)
            holding[i] = holding[i] + more
            rest = rest - more
    return np.array(holding)


def gaussian(own_key, dims, scale, most, pieces=(), held_as=jnp.bfloat16):
    gain = block_levels(own_key, dims, pieces, -0.22, 0.18) if pieces else 1.0
    entries = jax.random.normal(own_key, dims, jnp.float32) * scale * gain
    return jnp.minimum(jnp.maximum(entries, -most), most).astype(held_as)


def setup_inputs(seed: int = 0) -> dict:
    arg_keys = jax.random.split(jax.random.key(seed), 9)
    corona = gaussian(arg_keys[0], (FIELDS, NT, NP, NR), 1.0, 6.0, ((1, 4), (2, 8)), jnp.float32)
    kappa = jnp.clip(jnp.exp(math.log(1.0) - 2.9957323 * jax.random.uniform(arg_keys[1], (NT, NP, NR), jnp.float32) ** block_levels(arg_keys[1], (NT, NP, NR), ((0, 4), (1, 8)), -0.2, 0.2)), 0.05, 1.0)
    mixing = gaussian(arg_keys[2], (FIELDS, FIELDS), FIELDS ** -0.5, 2.0, (), jnp.float32)
    helio_prev = gaussian(arg_keys[3], (FIELDS, NFP, NFT), 1.0, 6.0, ((1, 8), (2, 4)), jnp.float32)
    owner_keys = jax.random.split(jax.random.fold_in(arg_keys[4], 1), TARGETS // T_DEV)
    owner_turns = jax.random.permutation(jax.random.fold_in(arg_keys[4], 3), TARGETS // T_DEV)
    owner = jax.vmap(lambda own, number: deal_out(jax.random.fold_in(arg_keys[4], 2), own, number, T_DEV, DEVICES, 1, CAP, 2))(owner_keys, owner_turns).reshape((TARGETS, 1))
    dest_cell = touch_ends(jax.random.randint(arg_keys[5], (TARGETS,), 0, FP * FT), jax.random.fold_in(arg_keys[5], 1), 0, (FP * FT) - 1).astype(jnp.int32)
    corner_base = draw_corner_base(jax.random.fold_in(arg_keys[8], 71), 0)
    fractions = jnp.clip(1.0 * jax.random.uniform(arg_keys[7], (3, TARGETS), jnp.float32) ** block_levels(arg_keys[7], (3, TARGETS), ((1, 32),), -0.2, 0.2), 0.0, 1.0)
    return {"corona": corona, "kappa": kappa, "mixing": mixing, "helio_prev": helio_prev, "owner": owner, "dest_cell": dest_cell, "corner_base": corner_base, "fractions": fractions}


def flux_step(field, cond, mixing):
    center = field[:, 1:-1, 1:-1, :]
    cond_c = cond[1:-1, 1:-1, :]
    radial = jnp.pad(center, ((0, 0), (0, 0), (0, 0), (1, 1)))
    cond_r = jnp.pad(cond_c, ((0, 0), (0, 0), (1, 1)))
    pairs = [(field[:, 2:, 1:-1, :], cond[2:, 1:-1, :]), (field[:, :-2, 1:-1, :], cond[:-2, 1:-1, :]),
             (field[:, 1:-1, 2:, :], cond[1:-1, 2:, :]), (field[:, 1:-1, :-2, :], cond[1:-1, :-2, :]),
             (radial[..., 2:], cond_r[..., 2:]), (radial[..., :-2], cond_r[..., :-2])]
    lapl = jnp.zeros_like(center)
    for near, cond_n in pairs:
        lapl = lapl + (0.5 * (cond_c + cond_n))[None] * (near - center)
    mixed = jnp.einsum("gf,fabr->gabr", mixing, center, precision=lax.Precision.HIGHEST)
    return center + 0.15 * lapl + 0.3 * mixed


def reference(corona, kappa, mixing, helio_prev, owner, dest_cell, corner_base, fractions):
    cond = jnp.pad(kappa, ((1, 1), (1, 1), (0, 0)))
    pad_spec = ((0, 0), (1, 1), (1, 1), (0, 0))
    first = flux_step(jnp.pad(corona, pad_spec), cond, mixing)
    stepped = flux_step(jnp.pad(first, pad_spec), cond, mixing)
    shell = stepped[:, :, :, NR - SH:]
    target = jnp.arange(TARGETS, dtype=jnp.int32)
    source = target // T_DEV
    src_lat = source // N_LON
    src_lon = source % N_LON
    t_idx = corner_base // (CP * SH)
    p_idx = (corner_base // SH) % CP
    r_idx = corner_base % SH
    g_lat = src_lat * CT + t_idx
    g_lon = src_lon * CP + p_idx
    value = jnp.zeros((FIELDS, TARGETS), jnp.float32)
    for a in range(2):
        for b in range(2):
            for c in range(2):
                weight = (fractions[0] if a else 1.0 - fractions[0]) * (fractions[1] if b else 1.0 - fractions[1]) * (fractions[2] if c else 1.0 - fractions[2])
                value = value + weight[None] * shell[:, g_lat + a, g_lon + b, r_idx + c]
    dest_owner = owner[:, 0]
    own_lat = dest_owner // N_LON
    own_lon = dest_owner % N_LON
    cell_p = dest_cell // FT
    cell_t = dest_cell % FT
    flat_idx = ((own_lon * FP + cell_p) * NFT + own_lat * FT + cell_t).astype(jnp.int32)
    added = jax.ops.segment_sum(value.T, flat_idx, num_segments=NFP * NFT)
    coupled = helio_prev + added.T.reshape(FIELDS, NFP, NFT)
    ext = jnp.pad(coupled, ((0, 0), (1, 1), (1, 1)))
    helio_face = coupled + 0.2 * (ext[:, 2:, 1:-1] + ext[:, :-2, 1:-1] + ext[:, 1:-1, 2:] + ext[:, 1:-1, :-2] - 4.0 * coupled)
    return stepped, helio_face
```

```python
import functools

import jax
import jax.numpy as jnp
from jax import lax
from jax.experimental import pallas as pl
from jax.experimental.pallas import tpu as pltpu
from jax.sharding import PartitionSpec as P

SH = 8
F32 = jnp.float32
BF16 = jnp.bfloat16
MESH = pl.DeviceIdType.MESH
LANES = 128
GROUP = 8
LAND = 4
NPAR = 5


def iota(shape, dim):
    return lax.broadcasted_iota(jnp.int32, shape, dim)


def split(x):
    hi = x.astype(BF16)
    return hi, (x - hi.astype(F32)).astype(BF16)


def dot_t(a, b):
    return lax.dot_general(a, b, (((1,), (1,)), ((), ())), preferred_element_type=F32)


def apply_step(c, near, kc, knear, mix):
    lane = iota(kc.shape, 1)
    last = kc.shape[1] - 1
    ks = [0.075 * (kc + kn) for kn in knear]
    kl = 0.075 * (kc + jnp.where(lane == 0, 0.0, pltpu.roll(kc, 1, 1)))
    kr = 0.075 * (kc + jnp.where(lane == last, 0.0, pltpu.roll(kc, last, 1)))
    diag = 1.0 - (((ks[0] + ks[1]) + (ks[2] + ks[3])) + (kl + kr))
    kl = jnp.where(lane == 0, 0.0, kl)
    kr = jnp.where(lane == last, 0.0, kr)
    total = diag[None] * c
    for k, u in zip(ks, near):
        total = total + k[None] * u
    total = total + kl[None] * pltpu.roll(c, 1, 2) + kr[None] * pltpu.roll(c, last, 2)
    out = []
    for g in range(c.shape[0]):
        row = total[g]
        for f in range(c.shape[0]):
            row = row + (0.3 * mix[g, f]) * c[f]
        out.append(row)
    return out


def shift_rows(c, low, high):
    n = c.shape[1]
    row = iota(c.shape, 1)
    down = jnp.where(row == 0, low, pltpu.roll(c, 1, 1))
    up = jnp.where(row == n - 1, high, pltpu.roll(c, n - 1, 1))
    return down, up


def kernel(
    n_lat, n_lon, corona, kappa, mix, helio, owner, dest, base, frac, stepped, face,
    ue, sp, pleft, pright, q2, cs, cr, first, fleft, fright, st, pk, ds, rd, vs, rv,
    shell, hs, hr, ts, tr, acc, load_sem, halo_send, halo_recv, out_sem,
    dest_send, dest_recv, val_send, val_recv, face_send, face_recv,
):
    n_dev = n_lat * n_lon
    fields = corona.shape[0]
    tt, pp = corona.shape[1], corona.shape[2]
    count = owner.shape[1]
    lat, lon = lax.axis_index("lat"), lax.axis_index("lon")
    me = lat * n_lon + lon

    loads = [
        pltpu.make_async_copy(corona, ue.at[0:fields, 2 : 2 + tt], load_sem.at[0]),
        pltpu.make_async_copy(kappa, ue.at[fields, 2 : 2 + tt], load_sem.at[1]),
    ]
    for copy in loads:
        copy.start()

    barrier = pltpu.get_barrier_semaphore()

    def greet(i, carry):
        o = lax.rem(me + i, n_dev)
        pl.semaphore_signal(
            barrier, inc=1, device_id=(lax.div(o, n_lon), lax.rem(o, n_lon)), device_id_type=MESH
        )
        return carry

    lax.fori_loop(1, n_dev, greet, 0)
    for copy in loads:
        copy.wait()

    for j, p in enumerate((0, 1, pp - 2, pp - 1)):
        sp[j] = ue[:, 2 : 2 + tt, p, :]
    corners = [(1, 1), (1, -1), (-1, 1), (-1, -1)]
    for k, (a, b) in enumerate(corners):
        t, p = (2 + tt - 1 if a > 0 else 2), (pp - 1 if b > 0 else 0)
        for f in range(fields + 1):
            cs[k, f : f + 1, :] = ue[f, t, p : p + 1, :]

    moves = [
        ((1, 0), ue.at[:, tt : tt + 2], ue.at[:, 0:2]),
        ((-1, 0), ue.at[:, 2:4], ue.at[:, tt + 2 : tt + 4]),
        ((0, 1), sp.at[3], pleft.at[:, 8 : 8 + tt]),
        ((0, 1), sp.at[2], q2.at[0]),
        ((0, -1), sp.at[0], pright.at[:, 8 : 8 + tt]),
        ((0, -1), sp.at[1], q2.at[1]),
    ] + [(ab, cs.at[k], cr.at[k]) for k, ab in enumerate(corners)]

    def inside(a, b):
        ok = lat >= 0
        if a > 0:
            ok = ok & (lat < n_lat - 1)
        if a < 0:
            ok = ok & (lat > 0)
        if b > 0:
            ok = ok & (lon < n_lon - 1)
        if b < 0:
            ok = ok & (lon > 0)
        return ok

    def remote(a, b, src, dst, send, recv):
        return pltpu.make_async_remote_copy(
            src_ref=src, dst_ref=dst, send_sem=send, recv_sem=recv,
            device_id=(lat + a, lon + b), device_id_type=MESH,
        )

    pl.semaphore_wait(barrier, n_dev - 1)
    for k, ((a, b), src, dst) in enumerate(moves):

        @pl.when(inside(a, b))
        def _(k=k, a=a, b=b, src=src, dst=dst):
            remote(a, b, src, dst, halo_send.at[k], halo_recv.at[k]).start()

        @pl.when(jnp.logical_not(inside(-a, -b)))
        def _(dst=dst):
            dst[...] = jnp.zeros(dst.shape, F32)

    own = owner[...]
    upper = (iota((LANES, LANES), 0) < iota((LANES, LANES), 1)).astype(F32).astype(BF16)
    carry = jnp.zeros((n_dev, 1), F32)
    ranks = []
    for blk in range(count // LANES):
        hit = jnp.where(
            iota((n_dev, LANES), 0) == own[:, blk * LANES : (blk + 1) * LANES], 1.0, 0.0
        )
        before = jnp.dot(hit.astype(BF16), upper, preferred_element_type=F32) + carry
        ranks.append(jnp.sum(hit * before, axis=0, keepdims=True))
        carry = carry + jnp.sum(hit, axis=1, keepdims=True)
    rank = jnp.concatenate(ranks, axis=1).astype(jnp.int32)
    rank_hot = jnp.where(iota((LANES, count), 0) == rank, 1.0, 0.0).astype(BF16)
    rows = [base[...].astype(F32)] + [frac[i : i + 1, :] for i in range(3)]
    rows.append((dest[...] + 1).astype(F32))
    pieces = []
    for row in rows:
        hi = row.astype(BF16).astype(F32)
        pieces += [hi, row - hi]
    chunk = 32

    def place(g, carry):
        mask = iota((chunk, count), 0) + g * chunk == own
        left = jnp.concatenate([jnp.where(mask, x, 0.0).astype(BF16) for x in pieces], axis=0)
        got = dot_t(left, rank_hot)
        for q in range(NPAR):
            val = got[2 * q * chunk : (2 * q + 1) * chunk] + got[(2 * q + 1) * chunk : (2 * q + 2) * chunk]
            for oc in range(chunk // GROUP):
                pk[g * (chunk // GROUP) + oc, q] = val[oc * GROUP : (oc + 1) * GROUP]
            if q == NPAR - 1:
                for o in range(chunk):
                    ds[g * chunk + o] = val[o : o + 1]
        return carry

    lax.fori_loop(0, n_dev // chunk, place, 0)

    def send_to(o, src, dst, send, recv):
        return pltpu.make_async_remote_copy(
            src_ref=src, dst_ref=dst, send_sem=send, recv_sem=recv,
            device_id=(lax.div(o, n_lon), lax.rem(o, n_lon)), device_id_type=MESH,
        )

    def send_dest(i, carry):
        o = lax.rem(me + i, n_dev)
        send_to(o, ds.at[o], rd.at[me], dest_send, dest_recv).start()
        return carry

    lax.fori_loop(1, n_dev, send_dest, 0)
    rd[me] = ds[me]

    for k, ((a, b), src, dst) in enumerate(moves):

        @pl.when(inside(-a, -b))
        def _(k=k, a=a, b=b, src=src, dst=dst):
            remote(-a, -b, src, dst, halo_send.at[k], halo_recv.at[k]).wait_recv()

    for k, (a, b) in enumerate(corners):
        side = pleft if b > 0 else pright
        row = 7 if a > 0 else 8 + tt
        for f in range(fields + 1):
            side[f, row : row + 1, :] = cr[k, f : f + 1, :]

    def first_row(i, carry):
        c = ue[:, i + 1]
        low, high = shift_rows(c, pleft[:, pl.ds(7 + i, 1), :], pright[:, pl.ds(7 + i, 1), :])
        up, down = ue[:, i], ue[:, i + 2]
        out = apply_step(
            c[:fields], [x[:fields] for x in (up, down, low, high)],
            c[fields], [x[fields] for x in (up, down, low, high)], mix,
        )
        off = ((i == 0) & (lat == 0)) | ((i == tt + 1) & (lat == n_lat - 1))
        keep = jnp.where(off, 0.0, 1.0)
        for g in range(fields):
            first[g, i] = out[g] * keep
        return carry

    lax.fori_loop(0, tt + 2, first_row, 0)
    for side, outer, inner, into, ok in (
        (pleft, q2.at[0], sp.at[0], fleft, lon > 0),
        (pright, q2.at[1], sp.at[3], fright, lon < n_lon - 1),
    ):
        near = [side[:, 7 : 7 + tt, :], side[:, 9 : 9 + tt, :], outer[...], inner[...]]
        c = side[:, 8 : 8 + tt, :]
        out = apply_step(c[:fields], [x[:fields] for x in near], c[fields], [x[fields] for x in near], mix)
        keep = jnp.where(ok, 1.0, 0.0)
        for g in range(fields):
            into[g] = out[g] * keep

    def second_row(t, carry):
        c = first[:, t + 1]
        low, high = shift_rows(c, fleft[:, pl.ds(t, 1), :], fright[:, pl.ds(t, 1), :])
        kc = ue[fields:, t + 2]
        klow, khigh = shift_rows(
            kc, pleft[fields:, pl.ds(8 + t, 1), :], pright[fields:, pl.ds(8 + t, 1), :]
        )
        out = apply_step(
            c, [first[:, t], first[:, t + 2], low, high],
            kc[0], [ue[fields, t + 1], ue[fields, t + 3], klow[0], khigh[0]], mix,
        )
        for g in range(fields):
            st[g, t] = out[g]
        return carry

    lax.fori_loop(0, tt, second_row, 0)
    write = pltpu.make_async_copy(st, stepped, out_sem)
    write.start()

    n_r = st.shape[3]

    def shell_row(t, carry):
        lane = iota((fields, LANES), 1)
        row = jnp.zeros((fields, LANES), F32)
        for p in range(pp):
            x = pltpu.roll(st[:, t, p, :], (p * SH + SH) % n_r, 1)
            row = jnp.where((lane >= p * SH) & (lane < (p + 1) * SH), x, row)
        shell[t] = row
        return carry

    lax.fori_loop(0, tt, shell_row, 0)
    s_hi, s_lo = split(shell[...].reshape(tt * fields, LANES))
    left = jnp.concatenate([s_hi, s_hi, s_lo], axis=1)
    groups = n_dev // GROUP
    wide = GROUP * LANES

    def values(i, carry):
        g = lax.rem(lax.div(me, GROUP) + i, groups)
        par = [
            jnp.concatenate([pk[g, q, k : k + 1, :] for k in range(GROUP)], axis=1)
            for q in range(NPAR - 1)
        ]
        cell = par[0].astype(jnp.int32)
        t0, p0, r0 = cell >> 7, (cell >> 3) & 15, cell & 7
        fx, fy, fz = par[1:]

        def weights(n, at, fr):
            idx = iota((n, wide), 0) - at
            return jnp.where(idx == 0, 1.0 - fr, jnp.where(idx == 1, fr, 0.0))

        wa, wb, wc = weights(tt, t0, fx), weights(pp, p0, fy), weights(SH, r0, fz)
        table = (wb[:, None, :] * wc[None]).reshape(pp * SH, wide)
        hi, lo = split(table)
        got = jnp.dot(left, jnp.concatenate([hi, lo, hi], axis=0), preferred_element_type=F32)
        val = jnp.sum(got.reshape(tt, fields, wide) * wa[:, None, :], axis=0)
        for k in range(GROUP):
            vs[g * GROUP + k] = val[:, k * LANES : (k + 1) * LANES]
        for k in range(GROUP):
            o = g * GROUP + k

            @pl.when(o != me)
            def _(o=o):
                send_to(o, vs.at[o], rv.at[me], val_send, val_recv).start()

        return carry

    lax.fori_loop(0, groups, values, 0)
    rv[me] = vs[me]

    other = lax.rem(me + 1, n_dev)
    all_dest = send_to(other, ds.at[0 : n_dev - 1], rd.at[0 : n_dev - 1], dest_send, dest_recv)
    all_vals = send_to(other, vs.at[0 : n_dev - 1], rv.at[0 : n_dev - 1], val_send, val_recv)
    all_dest.wait_recv()
    all_vals.wait_recv()

    face_p, face_t = helio.shape[1], helio.shape[2]
    acc[...] = jnp.zeros(acc.shape, F32)

    def land(i, carry):
        cell = jnp.concatenate([rd[i * LAND + k] for k in range(LAND)], axis=1).astype(jnp.int32) - 1
        val = jnp.concatenate([rv[i * LAND + k] for k in range(LAND)], axis=1)
        hi = val.astype(BF16).astype(F32)
        on_p = iota((face_p, LAND * LANES), 0) == (cell >> 7)
        on_t = jnp.where(iota((face_t, LAND * LANES), 0) == (cell & 127), 1.0, 0.0).astype(BF16)
        spread = jnp.concatenate(
            [jnp.where(on_p, x[f : f + 1], 0.0).astype(BF16) for x in (hi, val - hi) for f in range(fields)],
            axis=0,
        )
        acc[...] += dot_t(spread, on_t)
        return carry

    lax.fori_loop(0, n_dev // LAND, land, 0)
    half = fields * face_p
    flat = helio[...].reshape(half, face_t) + (acc[0:half] + acc[half:])
    coupled = flat.reshape(fields, face_p, face_t)

    for f in range(fields):
        hs[0, f : f + 1, :] = coupled[f, 0:1, :]
        hs[1, f : f + 1, :] = coupled[f, face_p - 1 : face_p, :]
    row8, lane8 = iota((8, face_t), 0), iota((8, face_t), 1)
    pick = jnp.where(
        ((row8 == 0) & (lane8 == 0)) | ((row8 == 1) & (lane8 == face_t - 1)), 1.0, 0.0
    )
    ts[...] = lax.dot_general(
        pick, flat, (((1,), (1,)), ((), ())), precision=lax.Precision.HIGHEST, preferred_element_type=F32
    )
    edges = [
        ((0, 1), hs.at[1], hr.at[0]),
        ((0, -1), hs.at[0], hr.at[1]),
        ((1, 0), ts, tr.at[0]),
        ((-1, 0), ts, tr.at[1]),
    ]
    for k, ((a, b), src, dst) in enumerate(edges):

        @pl.when(inside(a, b))
        def _(k=k, a=a, b=b, src=src, dst=dst):
            remote(a, b, src, dst, face_send.at[k], face_recv.at[k]).start()

        @pl.when(jnp.logical_not(inside(-a, -b)))
        def _(dst=dst):
            dst[...] = jnp.zeros(dst.shape, F32)

    lane3 = iota(coupled.shape, 2)
    inner = (
        jnp.where(lane3 == 0, 0.0, pltpu.roll(coupled, 1, 2))
        + jnp.where(lane3 == face_t - 1, 0.0, pltpu.roll(coupled, face_t - 1, 2))
        - 4.0 * coupled
    )
    for k, ((a, b), src, dst) in enumerate(edges):

        @pl.when(inside(-a, -b))
        def _(k=k, a=a, b=b, src=src, dst=dst):
            remote(-a, -b, src, dst, face_send.at[k], face_recv.at[k]).wait_recv()

    lows = jnp.concatenate([hr[0, f : f + 1, :][None] for f in range(fields)], axis=0)
    highs = jnp.concatenate([hr[1, f : f + 1, :][None] for f in range(fields)], axis=0)
    down, up = shift_rows(coupled, lows, highs)
    put_low = jnp.where((row8 == 1) & (lane8 == 0), 1.0, 0.0)
    put_high = jnp.where((row8 == 0) & (lane8 == face_t - 1), 1.0, 0.0)
    both = jnp.concatenate([tr[0], tr[1]], axis=0)
    sides = lax.dot_general(
        both, jnp.concatenate([put_low, put_high], axis=0), (((0,), (0,)), ((), ())),
        precision=lax.Precision.HIGHEST, preferred_element_type=F32,
    ).reshape(coupled.shape)
    face[...] = coupled + 0.2 * (inner + (down + up) + sides)

    for k, ((a, b), src, dst) in enumerate(moves):

        @pl.when(inside(a, b))
        def _(k=k, a=a, b=b, src=src, dst=dst):
            remote(a, b, src, dst, halo_send.at[k], halo_recv.at[k]).wait_send()

    for k, ((a, b), src, dst) in enumerate(edges):

        @pl.when(inside(a, b))
        def _(k=k, a=a, b=b, src=src, dst=dst):
            remote(a, b, src, dst, face_send.at[k], face_recv.at[k]).wait_send()

    all_dest.wait_send()
    all_vals.wait_send()
    write.wait()


def body(corona, kappa, mixing, helio_prev, owner, dest_cell, corner_base, fractions):
    n_lat, n_lon = lax.axis_size("lat"), lax.axis_size("lon")
    n_dev = n_lat * n_lon
    fields, tt, pp, n_r = corona.shape
    count = corner_base.shape[0]
    face_p, face_t = helio_prev.shape[1:]
    ext = fields + 1
    vmem = pl.BlockSpec(memory_space=pltpu.VMEM)
    hbm = pl.BlockSpec(memory_space=pl.ANY)
    sem = pltpu.SemaphoreType.DMA
    v = lambda *shape: pltpu.VMEM(shape, F32)
    return pl.pallas_call(
        functools.partial(kernel, n_lat, n_lon),
        out_shape=(
            jax.ShapeDtypeStruct(corona.shape, F32),
            jax.ShapeDtypeStruct(helio_prev.shape, F32),
        ),
        in_specs=[hbm, hbm, pl.BlockSpec(memory_space=pltpu.SMEM)] + [vmem] * 5,
        out_specs=(hbm, vmem),
        scratch_shapes=[
            v(ext, tt + 4, pp, n_r),
            v(4, ext, tt, n_r),
            v(ext, tt + 16, n_r),
            v(ext, tt + 16, n_r),
            v(2, ext, tt, n_r),
            v(4, 16, n_r),
            v(4, 16, n_r),
            v(fields, tt + 2, pp, n_r),
            v(fields, tt, n_r),
            v(fields, tt, n_r),
            v(fields, tt, pp, n_r),
            v(n_dev // GROUP, NPAR, GROUP, LANES),
            v(n_dev, 1, LANES),
            v(n_dev, 1, LANES),
            v(n_dev, fields, LANES),
            v(n_dev, fields, LANES),
            v(tt, fields, LANES),
            v(2, fields, face_t),
            v(2, fields, face_t),
            v(8, fields * face_p),
            v(2, 8, fields * face_p),
            v(2 * fields * face_p, face_t),
            sem((2,)), sem((10,)), sem((10,)), sem,
            sem, sem, sem, sem, sem((4,)), sem((4,)),
        ],
        compiler_params=pltpu.CompilerParams(
            collective_id=0, has_side_effects=True, vmem_limit_bytes=48 * 1024 * 1024
        ),
        name="corona_helio",
    )(
        corona, kappa, mixing, helio_prev, owner.reshape(1, count), dest_cell.reshape(1, count),
        corner_base.reshape(1, count), fractions,
    )


def solution(mesh):
    return jax.shard_map(
        body,
        mesh=mesh,
        in_specs=(
            P(None, "lat", "lon", None),
            P("lat", "lon", None),
            P(),
            P(None, "lon", "lat"),
            P(("lat", "lon"), None),
            P(("lat", "lon")),
            P(("lat", "lon")),
            P(None, ("lat", "lon")),
        ),
        out_specs=(P(None, "lat", "lon", None), P(None, "lon", "lat")),
        check_vma=False,
    )
```

```python
import functools

import jax
import jax.numpy as jnp
from jax import lax
from jax.experimental import pallas as pl
from jax.experimental.pallas import tpu as pltpu
from jax.sharding import PartitionSpec as P

SH = 8
F32 = jnp.float32
BF16 = jnp.bfloat16
MESH = pl.DeviceIdType.MESH
LANES = 128
GROUP = 8
LAND = 4
NPAR = 5


def iota(shape, dim):
    return lax.broadcasted_iota(jnp.int32, shape, dim)


def split(x):
    hi = x.astype(BF16)
    return hi, (x - hi.astype(F32)).astype(BF16)


def dot_t(a, b):
    return lax.dot_general(a, b, (((1,), (1,)), ((), ())), preferred_element_type=F32)


def apply_step(c, near, kc, knear, mix):
    lane = iota(kc.shape, 1)
    last = kc.shape[1] - 1
    ks = [0.075 * (kc + kn) for kn in knear]
    kl = 0.075 * (kc + jnp.where(lane == 0, 0.0, pltpu.roll(kc, 1, 1)))
    kr = 0.075 * (kc + jnp.where(lane == last, 0.0, pltpu.roll(kc, last, 1)))
    diag = 1.0 - (((ks[0] + ks[1]) + (ks[2] + ks[3])) + (kl + kr))
    kl = jnp.where(lane == 0, 0.0, kl)
    kr = jnp.where(lane == last, 0.0, kr)
    total = diag[None] * c
    for k, u in zip(ks, near):
        total = total + k[None] * u
    total = total + kl[None] * pltpu.roll(c, 1, 2) + kr[None] * pltpu.roll(c, last, 2)
    out = []
    for g in range(c.shape[0]):
        row = total[g]
        for f in range(c.shape[0]):
            row = row + (0.3 * mix[g, f]) * c[f]
        out.append(row)
    return out


def shift_rows(c, low, high):
    n = c.shape[1]
    row = iota(c.shape, 1)
    down = jnp.where(row == 0, low, pltpu.roll(c, 1, 1))
    up = jnp.where(row == n - 1, high, pltpu.roll(c, n - 1, 1))
    return down, up


def kernel(
    n_lat, n_lon, corona, kappa, mix_in, helio_in, owner_in, dest_in, base_in, frac_in, stepped, face_out,
    mix, helio, owner, dest, base, frac, face, ue, sp, pleft, pright, q2, cs, cr, first, fleft, fright, st, pk, ds, rd, vs, rv,
    shell, hs, hr, ts, tr, acc, load_sem, halo_send, halo_recv, out_sem, face_sem,
    dest_send, dest_recv, val_send, val_recv, face_send, face_recv,
):
    n_dev = n_lat * n_lon
    fields = corona.shape[0]
    tt, pp = corona.shape[1], corona.shape[2]
    count = owner.shape[1]
    lat, lon = lax.axis_index("lat"), lax.axis_index("lon")
    me = lat * n_lon + lon

    loads = [
        pltpu.make_async_copy(corona, ue.at[0:fields, 2 : 2 + tt], load_sem.at[0]),
        pltpu.make_async_copy(kappa, ue.at[fields, 2 : 2 + tt], load_sem.at[1]),
    ] + [
        pltpu.make_async_copy(src, dst, load_sem.at[2 + k])
        for k, (src, dst) in enumerate(
            ((owner_in, owner), (base_in, base), (frac_in, frac), (dest_in, dest), (mix_in, mix), (helio_in, helio))
        )
    ]
    for copy in loads:
        copy.start()

    barrier = pltpu.get_barrier_semaphore()

    def greet(i, carry):
        o = lax.rem(me + i, n_dev)
        pl.semaphore_signal(
            barrier, inc=1, device_id=(lax.div(o, n_lon), lax.rem(o, n_lon)), device_id_type=MESH
        )
        return carry

    lax.fori_loop(1, n_dev, greet, 0)
    for copy in loads[:2]:
        copy.wait()

    for j, p in enumerate((0, 1, pp - 2, pp - 1)):
        sp[j] = ue[:, 2 : 2 + tt, p, :]
    corners = [(1, 1), (1, -1), (-1, 1), (-1, -1)]
    for k, (a, b) in enumerate(corners):
        t, p = (2 + tt - 1 if a > 0 else 2), (pp - 1 if b > 0 else 0)
        for f in range(fields + 1):
            cs[k, f : f + 1, :] = ue[f, t, p : p + 1, :]

    moves = [
        ((1, 0), ue.at[:, tt : tt + 2], ue.at[:, 0:2]),
        ((-1, 0), ue.at[:, 2:4], ue.at[:, tt + 2 : tt + 4]),
        ((0, 1), sp.at[3], pleft.at[:, 8 : 8 + tt]),
        ((0, 1), sp.at[2], q2.at[0]),
        ((0, -1), sp.at[0], pright.at[:, 8 : 8 + tt]),
        ((0, -1), sp.at[1], q2.at[1]),
    ] + [(ab, cs.at[k], cr.at[k]) for k, ab in enumerate(corners)]

    def inside(a, b):
        ok = lat >= 0
        if a > 0:
            ok = ok & (lat < n_lat - 1)
        if a < 0:
            ok = ok & (lat > 0)
        if b > 0:
            ok = ok & (lon < n_lon - 1)
        if b < 0:
            ok = ok & (lon > 0)
        return ok

    def remote(a, b, src, dst, send, recv):
        return pltpu.make_async_remote_copy(
            src_ref=src, dst_ref=dst, send_sem=send, recv_sem=recv,
            device_id=(lat + a, lon + b), device_id_type=MESH,
        )

    pl.semaphore_wait(barrier, n_dev - 1)
    for k, ((a, b), src, dst) in enumerate(moves):

        @pl.when(inside(a, b))
        def _(k=k, a=a, b=b, src=src, dst=dst):
            remote(a, b, src, dst, halo_send.at[k], halo_recv.at[k]).start()

        @pl.when(jnp.logical_not(inside(-a, -b)))
        def _(dst=dst):
            dst[...] = jnp.zeros(dst.shape, F32)

    for copy in loads[2:]:
        copy.wait()

    own = owner[...]
    upper = (iota((LANES, LANES), 0) < iota((LANES, LANES), 1)).astype(F32).astype(BF16)
    carry = jnp.zeros((n_dev, 1), F32)
    ranks = []
    for blk in range(count // LANES):
        hit = jnp.where(
            iota((n_dev, LANES), 0) == own[:, blk * LANES : (blk + 1) * LANES], 1.0, 0.0
        )
        before = jnp.dot(hit.astype(BF16), upper, preferred_element_type=F32) + carry
        ranks.append(jnp.sum(hit * before, axis=0, keepdims=True))
        carry = carry + jnp.sum(hit, axis=1, keepdims=True)
    rank = jnp.concatenate(ranks, axis=1).astype(jnp.int32)
    rank_hot = jnp.where(iota((LANES, count), 0) == rank, 1.0, 0.0).astype(BF16)
    rows = [base[...].astype(F32)] + [frac[i : i + 1, :] for i in range(3)]
    rows.append((dest[...] + 1).astype(F32))
    pieces = []
    for row in rows:
        hi = row.astype(BF16).astype(F32)
        pieces += [hi, row - hi]
    chunk = 32

    def place(g, carry):
        mask = iota((chunk, count), 0) + g * chunk == own
        left = jnp.concatenate([jnp.where(mask, x, 0.0).astype(BF16) for x in pieces], axis=0)
        got = dot_t(left, rank_hot)
        for q in range(NPAR):
            val = got[2 * q * chunk : (2 * q + 1) * chunk] + got[(2 * q + 1) * chunk : (2 * q + 2) * chunk]
            for oc in range(chunk // GROUP):
                pk[g * (chunk // GROUP) + oc, q] = val[oc * GROUP : (oc + 1) * GROUP]
            if q == NPAR - 1:
                for o in range(chunk):
                    ds[g * chunk + o] = val[o : o + 1]
        return carry

    lax.fori_loop(0, n_dev // chunk, place, 0)

    def send_to(o, src, dst, send, recv):
        return pltpu.make_async_remote_copy(
            src_ref=src, dst_ref=dst, send_sem=send, recv_sem=recv,
            device_id=(lax.div(o, n_lon), lax.rem(o, n_lon)), device_id_type=MESH,
        )

    def send_dest(i, carry):
        o = lax.rem(me + i, n_dev)
        send_to(o, ds.at[o], rd.at[me], dest_send, dest_recv).start()
        return carry

    lax.fori_loop(1, n_dev, send_dest, 0)
    rd[me] = ds[me]

    for k, ((a, b), src, dst) in enumerate(moves):

        @pl.when(inside(-a, -b))
        def _(k=k, a=a, b=b, src=src, dst=dst):
            remote(-a, -b, src, dst, halo_send.at[k], halo_recv.at[k]).wait_recv()

    for k, (a, b) in enumerate(corners):
        side = pleft if b > 0 else pright
        row = 7 if a > 0 else 8 + tt
        for f in range(fields + 1):
            side[f, row : row + 1, :] = cr[k, f : f + 1, :]

    def first_row(i, carry):
        c = ue[:, i + 1]
        low, high = shift_rows(c, pleft[:, pl.ds(7 + i, 1), :], pright[:, pl.ds(7 + i, 1), :])
        up, down = ue[:, i], ue[:, i + 2]
        out = apply_step(
            c[:fields], [x[:fields] for x in (up, down, low, high)],
            c[fields], [x[fields] for x in (up, down, low, high)], mix,
        )
        off = ((i == 0) & (lat == 0)) | ((i == tt + 1) & (lat == n_lat - 1))
        keep = jnp.where(off, 0.0, 1.0)
        for g in range(fields):
            first[g, i] = out[g] * keep
        return carry

    lax.fori_loop(0, tt + 2, first_row, 0)
    for side, outer, inner, into, ok in (
        (pleft, q2.at[0], sp.at[0], fleft, lon > 0),
        (pright, q2.at[1], sp.at[3], fright, lon < n_lon - 1),
    ):
        near = [side[:, 7 : 7 + tt, :], side[:, 9 : 9 + tt, :], outer[...], inner[...]]
        c = side[:, 8 : 8 + tt, :]
        out = apply_step(c[:fields], [x[:fields] for x in near], c[fields], [x[fields] for x in near], mix)
        keep = jnp.where(ok, 1.0, 0.0)
        for g in range(fields):
            into[g] = out[g] * keep

    def second_row(t, carry):
        c = first[:, t + 1]
        low, high = shift_rows(c, fleft[:, pl.ds(t, 1), :], fright[:, pl.ds(t, 1), :])
        kc = ue[fields:, t + 2]
        klow, khigh = shift_rows(
            kc, pleft[fields:, pl.ds(8 + t, 1), :], pright[fields:, pl.ds(8 + t, 1), :]
        )
        out = apply_step(
            c, [first[:, t], first[:, t + 2], low, high],
            kc[0], [ue[fields, t + 1], ue[fields, t + 3], klow[0], khigh[0]], mix,
        )
        for g in range(fields):
            st[g, t] = out[g]
        return carry

    lax.fori_loop(0, tt, second_row, 0)
    write = pltpu.make_async_copy(st, stepped, out_sem)
    write.start()

    n_r = st.shape[3]

    def shell_row(t, carry):
        lane = iota((fields, LANES), 1)
        row = jnp.zeros((fields, LANES), F32)
        for p in range(pp):
            x = pltpu.roll(st[:, t, p, :], (p * SH + SH) % n_r, 1)
            row = jnp.where((lane >= p * SH) & (lane < (p + 1) * SH), x, row)
        shell[t] = row
        return carry

    lax.fori_loop(0, tt, shell_row, 0)
    s_hi, s_lo = split(shell[...].reshape(tt * fields, LANES))
    left = jnp.concatenate([s_hi, s_hi, s_lo], axis=1)
    groups = n_dev // GROUP
    wide = GROUP * LANES

    def values(i, carry):
        g = lax.rem(lax.div(me, GROUP) + i, groups)
        par = [
            jnp.concatenate([pk[g, q, k : k + 1, :] for k in range(GROUP)], axis=1)
            for q in range(NPAR - 1)
        ]
        cell = par[0].astype(jnp.int32)
        t0, p0, r0 = cell >> 7, (cell >> 3) & 15, cell & 7
        fx, fy, fz = par[1:]

        def weights(n, at, fr):
            idx = iota((n, wide), 0) - at
            return jnp.where(idx == 0, 1.0 - fr, jnp.where(idx == 1, fr, 0.0))

        wa, wb, wc = weights(tt, t0, fx), weights(pp, p0, fy), weights(SH, r0, fz)
        table = (wb[:, None, :] * wc[None]).reshape(pp * SH, wide)
        hi, lo = split(table)
        got = jnp.dot(left, jnp.concatenate([hi, lo, hi], axis=0), preferred_element_type=F32)
        val = jnp.sum(got.reshape(tt, fields, wide) * wa[:, None, :], axis=0)
        for k in range(GROUP):
            vs[g * GROUP + k] = val[:, k * LANES : (k + 1) * LANES]
        for k in range(GROUP):
            o = g * GROUP + k

            @pl.when(o != me)
            def _(o=o):
                send_to(o, vs.at[o], rv.at[me], val_send, val_recv).start()

        return carry

    lax.fori_loop(0, groups, values, 0)
    rv[me] = vs[me]

    other = lax.rem(me + 1, n_dev)
    all_dest = send_to(other, ds.at[0 : n_dev - 1], rd.at[0 : n_dev - 1], dest_send, dest_recv)
    all_vals = send_to(other, vs.at[0 : n_dev - 1], rv.at[0 : n_dev - 1], val_send, val_recv)
    all_dest.wait_recv()
    all_vals.wait_recv()

    face_p, face_t = helio.shape[1], helio.shape[2]
    acc[...] = jnp.zeros(acc.shape, F32)

    def land(i, carry):
        cell = jnp.concatenate([rd[i * LAND + k] for k in range(LAND)], axis=1).astype(jnp.int32) - 1
        val = jnp.concatenate([rv[i * LAND + k] for k in range(LAND)], axis=1)
        hi = val.astype(BF16).astype(F32)
        on_p = iota((face_p, LAND * LANES), 0) == (cell >> 7)
        on_t = jnp.where(iota((face_t, LAND * LANES), 0) == (cell & 127), 1.0, 0.0).astype(BF16)
        spread = jnp.concatenate(
            [jnp.where(on_p, x[f : f + 1], 0.0).astype(BF16) for x in (hi, val - hi) for f in range(fields)],
            axis=0,
        )
        acc[...] += dot_t(spread, on_t)
        return carry

    lax.fori_loop(0, n_dev // LAND, land, 0)
    half = fields * face_p
    flat = helio[...].reshape(half, face_t) + (acc[0:half] + acc[half:])
    coupled = flat.reshape(fields, face_p, face_t)

    for f in range(fields):
        hs[0, f : f + 1, :] = coupled[f, 0:1, :]
        hs[1, f : f + 1, :] = coupled[f, face_p - 1 : face_p, :]
    row8, lane8 = iota((8, face_t), 0), iota((8, face_t), 1)
    pick = jnp.where(
        ((row8 == 0) & (lane8 == 0)) | ((row8 == 1) & (lane8 == face_t - 1)), 1.0, 0.0
    )
    ts[...] = lax.dot_general(
        pick, flat, (((1,), (1,)), ((), ())), precision=lax.Precision.HIGHEST, preferred_element_type=F32
    )
    edges = [
        ((0, 1), hs.at[1], hr.at[0]),
        ((0, -1), hs.at[0], hr.at[1]),
        ((1, 0), ts, tr.at[0]),
        ((-1, 0), ts, tr.at[1]),
    ]
    for k, ((a, b), src, dst) in enumerate(edges):

        @pl.when(inside(a, b))
        def _(k=k, a=a, b=b, src=src, dst=dst):
            remote(a, b, src, dst, face_send.at[k], face_recv.at[k]).start()

        @pl.when(jnp.logical_not(inside(-a, -b)))
        def _(dst=dst):
            dst[...] = jnp.zeros(dst.shape, F32)

    lane3 = iota(coupled.shape, 2)
    inner = (
        jnp.where(lane3 == 0, 0.0, pltpu.roll(coupled, 1, 2))
        + jnp.where(lane3 == face_t - 1, 0.0, pltpu.roll(coupled, face_t - 1, 2))
        - 4.0 * coupled
    )
    for k, ((a, b), src, dst) in enumerate(edges):

        @pl.when(inside(-a, -b))
        def _(k=k, a=a, b=b, src=src, dst=dst):
            remote(-a, -b, src, dst, face_send.at[k], face_recv.at[k]).wait_recv()

    lows = jnp.concatenate([hr[0, f : f + 1, :][None] for f in range(fields)], axis=0)
    highs = jnp.concatenate([hr[1, f : f + 1, :][None] for f in range(fields)], axis=0)
    down, up = shift_rows(coupled, lows, highs)
    put_low = jnp.where((row8 == 1) & (lane8 == 0), 1.0, 0.0)
    put_high = jnp.where((row8 == 0) & (lane8 == face_t - 1), 1.0, 0.0)
    both = jnp.concatenate([tr[0], tr[1]], axis=0)
    sides = lax.dot_general(
        both, jnp.concatenate([put_low, put_high], axis=0), (((0,), (0,)), ((), ())),
        precision=lax.Precision.HIGHEST, preferred_element_type=F32,
    ).reshape(coupled.shape)
    face[...] = coupled + 0.2 * (inner + (down + up) + sides)
    write_face = pltpu.make_async_copy(face, face_out, face_sem)
    write_face.start()

    for k, ((a, b), src, dst) in enumerate(moves):

        @pl.when(inside(a, b))
        def _(k=k, a=a, b=b, src=src, dst=dst):
            remote(a, b, src, dst, halo_send.at[k], halo_recv.at[k]).wait_send()

    for k, ((a, b), src, dst) in enumerate(edges):

        @pl.when(inside(a, b))
        def _(k=k, a=a, b=b, src=src, dst=dst):
            remote(a, b, src, dst, face_send.at[k], face_recv.at[k]).wait_send()

    all_dest.wait_send()
    all_vals.wait_send()
    write.wait()
    write_face.wait()


def body(corona, kappa, mixing, helio_prev, owner, dest_cell, corner_base, fractions):
    n_lat, n_lon = lax.axis_size("lat"), lax.axis_size("lon")
    n_dev = n_lat * n_lon
    fields, tt, pp, n_r = corona.shape
    count = corner_base.shape[0]
    face_p, face_t = helio_prev.shape[1:]
    ext = fields + 1
    hbm = pl.BlockSpec(memory_space=pl.ANY)
    sem = pltpu.SemaphoreType.DMA
    v = lambda *shape: pltpu.VMEM(shape, F32)
    return pl.pallas_call(
        functools.partial(kernel, n_lat, n_lon),
        out_shape=(
            jax.ShapeDtypeStruct(corona.shape, F32),
            jax.ShapeDtypeStruct(helio_prev.shape, F32),
        ),
        in_specs=[hbm] * 8,
        out_specs=(hbm, hbm),
        scratch_shapes=[
            pltpu.SMEM(mixing.shape, F32),
            v(*helio_prev.shape),
            pltpu.VMEM((1, count), jnp.int32),
            pltpu.VMEM((1, count), jnp.int32),
            pltpu.VMEM((1, count), jnp.int32),
            v(3, count),
            v(*helio_prev.shape),
            v(ext, tt + 4, pp, n_r),
            v(4, ext, tt, n_r),
            v(ext, tt + 16, n_r),
            v(ext, tt + 16, n_r),
            v(2, ext, tt, n_r),
            v(4, 16, n_r),
            v(4, 16, n_r),
            v(fields, tt + 2, pp, n_r),
            v(fields, tt, n_r),
            v(fields, tt, n_r),
            v(fields, tt, pp, n_r),
            v(n_dev // GROUP, NPAR, GROUP, LANES),
            v(n_dev, 1, LANES),
            v(n_dev, 1, LANES),
            v(n_dev, fields, LANES),
            v(n_dev, fields, LANES),
            v(tt, fields, LANES),
            v(2, fields, face_t),
            v(2, fields, face_t),
            v(8, fields * face_p),
            v(2, 8, fields * face_p),
            v(2 * fields * face_p, face_t),
            sem((8,)), sem((10,)), sem((10,)), sem, sem,
            sem, sem, sem, sem, sem((4,)), sem((4,)),
        ],
        compiler_params=pltpu.CompilerParams(
            collective_id=0, has_side_effects=True, vmem_limit_bytes=63 * 1024 * 1024
        ),
        name="corona_helio",
    )(
        corona, kappa, mixing, helio_prev, owner.reshape(1, count), dest_cell.reshape(1, count),
        corner_base.reshape(1, count), fractions,
    )


def solution(mesh):
    return jax.shard_map(
        body,
        mesh=mesh,
        in_specs=(
            P(None, "lat", "lon", None),
            P("lat", "lon", None),
            P(),
            P(None, "lon", "lat"),
            P(("lat", "lon"), None),
            P(("lat", "lon")),
            P(("lat", "lon")),
            P(None, ("lat", "lon")),
        ),
        out_specs=(P(None, "lat", "lon", None), P(None, "lon", "lat")),
        check_vma=False,
    )
```

```python
import functools

import jax
import jax.numpy as jnp
from jax import lax
from jax.experimental import pallas as pl
from jax.experimental.pallas import tpu as pltpu
from jax.sharding import PartitionSpec as P

SH = 8
F32 = jnp.float32
BF16 = jnp.bfloat16
MESH = pl.DeviceIdType.MESH
LANES = 128
GROUP = 8
LAND = 4
NPAR = 5
DEEP = 16
WIDE = 4 * LANES


def iota(shape, dim):
    return lax.broadcasted_iota(jnp.int32, shape, dim)


def split(x):
    hi = x.astype(BF16)
    return hi, (x - hi.astype(F32)).astype(BF16)


def dot_t(a, b):
    return lax.dot_general(a, b, (((1,), (1,)), ((), ())), preferred_element_type=F32)


def apply_step(c, near, kc, knear, mix):
    lane = iota(kc.shape, 1)
    last = kc.shape[1] - 1
    ks = [0.075 * (kc + kn) for kn in knear]
    kl = 0.075 * (kc + jnp.where(lane == 0, 0.0, pltpu.roll(kc, 1, 1)))
    kr = 0.075 * (kc + jnp.where(lane == last, 0.0, pltpu.roll(kc, last, 1)))
    diag = 1.0 - (((ks[0] + ks[1]) + (ks[2] + ks[3])) + (kl + kr))
    kl = jnp.where(lane == 0, 0.0, kl)
    kr = jnp.where(lane == last, 0.0, kr)
    total = diag[None] * c
    for k, u in zip(ks, near):
        total = total + k[None] * u
    total = total + kl[None] * pltpu.roll(c, 1, 2) + kr[None] * pltpu.roll(c, last, 2)
    out = []
    for g in range(c.shape[0]):
        row = total[g]
        for f in range(c.shape[0]):
            row = row + (0.3 * mix[g, f]) * c[f]
        out.append(row)
    return out


def shift_rows(c, low, high):
    n = c.shape[1]
    row = iota(c.shape, 1)
    down = jnp.where(row == 0, low, pltpu.roll(c, 1, 1))
    up = jnp.where(row == n - 1, high, pltpu.roll(c, n - 1, 1))
    return down, up


def kernel(
    n_lat, n_lon, corona, kappa, mix_in, helio_in, owner_in, dest_in, base_in, frac_in, stepped, face_out,
    mix, mixv, helio, owner, dest, base, frac, face, xe, ke, xm, xf, co, ue, sp, pleft, pright, q2, cs, cr, first, fleft, fright, st, pk, ds, rd, vs, rv,
    shell, hs, hr, ts, tr, acc, load_sem, halo_send, halo_recv, small_send, small_recv, out_sem, face_sem,
    dest_send, dest_recv, val_send, val_recv, face_send, face_recv,
):
    n_dev = n_lat * n_lon
    fields = corona.shape[0]
    tt, pp = corona.shape[1], corona.shape[2]
    count = owner.shape[1]
    lat, lon = lax.axis_index("lat"), lax.axis_index("lon")
    me = lat * n_lon + lon

    loads = [
        pltpu.make_async_copy(corona, ue.at[0:fields, 2 : 2 + tt], load_sem.at[0]),
        pltpu.make_async_copy(kappa, ue.at[fields, 2 : 2 + tt], load_sem.at[1]),
    ] + [
        pltpu.make_async_copy(src, dst, load_sem.at[2 + k])
        for k, (src, dst) in enumerate(
            ((owner_in, owner), (base_in, base), (frac_in, frac), (dest_in, dest), (mix_in, mix), (mix_in, mixv), (helio_in, helio))
        )
    ]
    for copy in loads:
        copy.start()

    barrier = pltpu.get_barrier_semaphore()

    def greet(i, carry):
        o = lax.rem(me + i, n_dev)
        pl.semaphore_signal(
            barrier, inc=1, device_id=(lax.div(o, n_lon), lax.rem(o, n_lon)), device_id_type=MESH
        )
        return carry

    lax.fori_loop(1, n_dev, greet, 0)
    for copy in loads[:2]:
        copy.wait()

    per = LANES // DEEP
    lane1 = iota((1, LANES), 1)

    def extract(t, carry):
        lane = iota((fields, LANES), 1) // DEEP
        for h in range(pp // per):
            row = jnp.zeros((fields, LANES), F32)
            for j in range(per):
                x = pltpu.roll(ue[0:fields, t + 2, h * per + j, :], (j + 1) * DEEP % LANES, 1)
                row = jnp.where(lane == j, x, row)
            xe[t + 2, :, (h + 1) * LANES : (h + 2) * LANES] = row
        return carry

    lax.fori_loop(0, tt, extract, 0)
    lane_t = iota((tt, LANES), 1) // DEEP
    for h in range(pp // per):
        row = jnp.zeros((tt, LANES), F32)
        for j in range(per):
            x = pltpu.roll(ue[fields, 2 : 2 + tt, h * per + j, :], (j + 1) * DEEP % LANES, 1)
            row = jnp.where(lane_t == j, x, row)
        ke[2 : 2 + tt, :, (h + 1) * LANES : (h + 2) * LANES] = row[:, None, :]
    for ref in (xe, ke):
        for t in (0, tt + 3):
            for lo in (0, WIDE - LANES):
                ref[t, :, lo : lo + LANES] = jnp.zeros((ref.shape[1], LANES), F32)

    corners = [(1, 1), (1, -1), (-1, 1), (-1, -1)]
    moves = [
        ((1, 0), ue.at[:, tt : tt + 2], ue.at[:, 0:2]),
        ((-1, 0), ue.at[:, 2:4], ue.at[:, tt + 2 : tt + 4]),
        ((0, 1), sp.at[3], pleft.at[:, 8 : 8 + tt]),
        ((0, 1), sp.at[2], q2.at[0]),
        ((0, -1), sp.at[0], pright.at[:, 8 : 8 + tt]),
        ((0, -1), sp.at[1], q2.at[1]),
    ] + [(ab, cs.at[k], cr.at[k]) for k, ab in enumerate(corners)]

    mid = slice(LANES, WIDE - LANES)
    rows_in = slice(2, 2 + tt)
    places = [
        ((1, 0), (slice(tt, tt + 2), mid), (slice(0, 2), mid)),
        ((-1, 0), (slice(2, 4), mid), (slice(tt + 2, tt + 4), mid)),
        ((0, 1), (rows_in, slice(2 * LANES, 3 * LANES)), (rows_in, slice(0, LANES))),
        ((0, -1), (rows_in, slice(LANES, 2 * LANES)), (rows_in, slice(3 * LANES, WIDE))),
    ]
    for a, b in corners:
        src_t = slice(tt + 1, tt + 2) if a > 0 else slice(2, 3)
        dst_t = slice(1, 2) if a > 0 else slice(tt + 2, tt + 3)
        src_l = slice(2 * LANES, 3 * LANES) if b > 0 else slice(LANES, 2 * LANES)
        dst_l = slice(0, LANES) if b > 0 else slice(3 * LANES, WIDE)
        places.append(((a, b), (src_t, src_l), (dst_t, dst_l)))
    small = [
        (ab, ref.at[src[0], :, src[1]], ref.at[dst[0], :, dst[1]])
        for ab, src, dst in places
        for ref in (xe, ke)
    ]

    def inside(a, b):
        ok = lat >= 0
        if a > 0:
            ok = ok & (lat < n_lat - 1)
        if a < 0:
            ok = ok & (lat > 0)
        if b > 0:
            ok = ok & (lon < n_lon - 1)
        if b < 0:
            ok = ok & (lon > 0)
        return ok

    def remote(a, b, src, dst, send, recv):
        return pltpu.make_async_remote_copy(
            src_ref=src, dst_ref=dst, send_sem=send, recv_sem=recv,
            device_id=(lat + a, lon + b), device_id_type=MESH,
        )

    def launch(todo, send, recv):
        for k, ((a, b), src, dst) in enumerate(todo):

            @pl.when(inside(a, b))
            def _(k=k, a=a, b=b, src=src, dst=dst):
                remote(a, b, src, dst, send.at[k], recv.at[k]).start()

            @pl.when(jnp.logical_not(inside(-a, -b)))
            def _(dst=dst):
                dst[...] = jnp.zeros(dst.shape, F32)

    def arrive(todo, send, recv):
        for k, ((a, b), src, dst) in enumerate(todo):

            @pl.when(inside(-a, -b))
            def _(k=k, a=a, b=b, src=src, dst=dst):
                remote(-a, -b, src, dst, send.at[k], recv.at[k]).wait_recv()

    def leave(todo, send, recv):
        for k, ((a, b), src, dst) in enumerate(todo):

            @pl.when(inside(a, b))
            def _(k=k, a=a, b=b, src=src, dst=dst):
                remote(a, b, src, dst, send.at[k], recv.at[k]).wait_send()

    pl.semaphore_wait(barrier, n_dev - 1)
    launch(small, small_send, small_recv)
    for j, p in enumerate((0, 1, pp - 2, pp - 1)):
        sp[j] = ue[:, 2 : 2 + tt, p, :]
    for k, (a, b) in enumerate(corners):
        t, p = (2 + tt - 1 if a > 0 else 2), (pp - 1 if b > 0 else 0)
        for f in range(fields + 1):
            cs[k, f : f + 1, :] = ue[f, t, p : p + 1, :]

    launch(moves, halo_send, halo_recv)

    for copy in loads[2:]:
        copy.wait()

    own = owner[...]
    upper = (iota((LANES, LANES), 0) < iota((LANES, LANES), 1)).astype(F32).astype(BF16)
    carry = jnp.zeros((n_dev, 1), F32)
    ranks = []
    for blk in range(count // LANES):
        hit = jnp.where(
            iota((n_dev, LANES), 0) == own[:, blk * LANES : (blk + 1) * LANES], 1.0, 0.0
        )
        before = jnp.dot(hit.astype(BF16), upper, preferred_element_type=F32) + carry
        ranks.append(jnp.sum(hit * before, axis=0, keepdims=True))
        carry = carry + jnp.sum(hit, axis=1, keepdims=True)
    rank = jnp.concatenate(ranks, axis=1).astype(jnp.int32)
    rank_hot = jnp.where(iota((LANES, count), 0) == rank, 1.0, 0.0).astype(BF16)
    rows = [base[...].astype(F32)] + [frac[i : i + 1, :] for i in range(3)]
    rows.append((dest[...] + 1).astype(F32))
    pieces = []
    for row in rows:
        hi = row.astype(BF16).astype(F32)
        pieces += [hi, row - hi]
    chunk = 32

    def place(g, carry):
        mask = iota((chunk, count), 0) + g * chunk == own
        left = jnp.concatenate([jnp.where(mask, x, 0.0).astype(BF16) for x in pieces], axis=0)
        got = dot_t(left, rank_hot)
        for q in range(NPAR):
            val = got[2 * q * chunk : (2 * q + 1) * chunk] + got[(2 * q + 1) * chunk : (2 * q + 2) * chunk]
            for oc in range(chunk // GROUP):
                pk[g * (chunk // GROUP) + oc, q] = val[oc * GROUP : (oc + 1) * GROUP]
            if q == NPAR - 1:
                for o in range(chunk):
                    ds[g * chunk + o] = val[o : o + 1]
        return carry

    lax.fori_loop(0, n_dev // chunk, place, 0)

    def send_to(o, src, dst, send, recv):
        return pltpu.make_async_remote_copy(
            src_ref=src, dst_ref=dst, send_sem=send, recv_sem=recv,
            device_id=(lax.div(o, n_lon), lax.rem(o, n_lon)), device_id_type=MESH,
        )

    def send_dest(i, carry):
        o = lax.rem(me + i, n_dev)
        send_to(o, ds.at[o], rd.at[me], dest_send, dest_recv).start()
        return carry

    lax.fori_loop(1, n_dev, send_dest, 0)
    rd[me] = ds[me]

    nrow = (tt + 2) * fields
    hot = jnp.where(iota((nrow, fields), 0) % fields == iota((nrow, fields), 1), 1.0, 0.0)
    wide_mix = lax.dot_general(
        jnp.dot(hot, 0.3 * mixv[...], precision=lax.Precision.HIGHEST, preferred_element_type=F32),
        hot, (((1,), (1,)), ((), ())), precision=lax.Precision.HIGHEST, preferred_element_type=F32,
    )
    same = iota((nrow, nrow), 0) // fields == iota((nrow, nrow), 1) // fields
    m_hi, m_lo = split(jnp.where(same, wide_mix, 0.0))

    def mixed(x, n):
        hi, lo = split(x)
        mh, ml = m_hi[:n, :n], m_lo[:n, :n]
        dot = lambda a, b: jnp.dot(a, b, preferred_element_type=F32)
        return dot(mh, hi) + (dot(mh, lo) + dot(ml, hi))

    arrive(small, small_send, small_recv)
    xm[...] = mixed(xe[1 : tt + 3].reshape(nrow, WIDE), nrow).reshape(tt + 2, fields, WIDE)
    lane = iota((1, WIDE), 1)
    top = lane % DEEP == DEEP - 1
    outside = ((lane < LANES) & (lon == 0)) | ((lane >= WIDE - LANES) & (lon == n_lon - 1))
    keep_lane = jnp.where(outside, 0.0, 1.0)

    def roll(x, by):
        return pltpu.roll(x, by % WIDE, 1)

    def compact_row(c, up, down, k, more):
        return (
            more + k[6] * c + (k[0] * up + k[1] * down) + (k[2] * roll(c, DEEP) + k[3] * roll(c, -DEEP))
            + (k[4] * roll(c, 1) + k[5] * roll(c, -1))
        )

    def compact_first(i, carry):
        kc = ke[i + 1]
        k = [0.075 * (kc + x) for x in (ke[i], ke[i + 2], roll(kc, DEEP), roll(kc, -DEEP), roll(kc, 1))]
        outer = 0.075 * (kc + jnp.where(top, 0.0, roll(kc, -1)))
        diag = 1.0 - (((k[0] + k[1]) + (k[2] + k[3])) + (k[4] + outer))
        k += [jnp.where(top, 0.0, outer), diag]
        off = ((i == 0) & (lat == 0)) | ((i == tt + 1) & (lat == n_lat - 1))
        keep = keep_lane * jnp.where(off, 0.0, 1.0)
        xf[i] = keep * compact_row(xe[i + 1], xe[i], xe[i + 2], k, xm[i])

        @pl.when((i > 0) & (i < tt + 1))
        def _():
            for q in range(7):
                co[i - 1, q] = k[q]

        return carry

    lax.fori_loop(0, tt + 2, compact_first, 0)
    xm[0:tt] = mixed(xf[1 : tt + 1].reshape(tt * fields, WIDE), tt * fields).reshape(tt, fields, WIDE)

    def compact_second(t, carry):
        out = compact_row(xf[t + 1], xf[t], xf[t + 2], [co[t, q] for q in range(7)], xm[t])
        shell[t] = out[:, mid]
        return carry

    lax.fori_loop(0, tt, compact_second, 0)
    deep_at, cell_at = iota((2 * LANES, LANES), 0), iota((2 * LANES, LANES), 1)
    take = jnp.where(
        (deep_at // DEEP == cell_at // SH) & (deep_at % DEEP == cell_at % SH + DEEP - SH), 1.0, 0.0
    ).astype(BF16)
    s_hi, s_lo = [
        jnp.dot(x, take, preferred_element_type=F32).astype(BF16)
        for x in split(shell[...].reshape(tt * fields, 2 * LANES))
    ]
    left = jnp.concatenate([s_hi, s_hi, s_lo], axis=1)
    groups = n_dev // GROUP
    wide = GROUP * LANES

    def values(i, carry):
        g = lax.rem(lax.div(me, GROUP) + i, groups)
        par = [
            jnp.concatenate([pk[g, q, k : k + 1, :] for k in range(GROUP)], axis=1)
            for q in range(NPAR - 1)
        ]
        cell = par[0].astype(jnp.int32)
        t0, p0, r0 = cell >> 7, (cell >> 3) & 15, cell & 7
        fx, fy, fz = par[1:]

        def weights(n, at, fr):
            idx = iota((n, wide), 0) - at
            return jnp.where(idx == 0, 1.0 - fr, jnp.where(idx == 1, fr, 0.0))

        wa, wb, wc = weights(tt, t0, fx), weights(pp, p0, fy), weights(SH, r0, fz)
        table = (wb[:, None, :] * wc[None]).reshape(pp * SH, wide)
        hi, lo = split(table)
        got = jnp.dot(left, jnp.concatenate([hi, lo, hi], axis=0), preferred_element_type=F32)
        val = jnp.sum(got.reshape(tt, fields, wide) * wa[:, None, :], axis=0)
        for k in range(GROUP):
            vs[g * GROUP + k] = val[:, k * LANES : (k + 1) * LANES]
        for k in range(GROUP):
            o = g * GROUP + k

            @pl.when(o != me)
            def _(o=o):
                send_to(o, vs.at[o], rv.at[me], val_send, val_recv).start()

        return carry

    lax.fori_loop(0, groups, values, 0)
    rv[me] = vs[me]

    arrive(moves, halo_send, halo_recv)
    for k, (a, b) in enumerate(corners):
        side = pleft if b > 0 else pright
        row = 7 if a > 0 else 8 + tt
        for f in range(fields + 1):
            side[f, row : row + 1, :] = cr[k, f : f + 1, :]

    def first_row(i, carry):
        c = ue[:, i + 1]
        low, high = shift_rows(c, pleft[:, pl.ds(7 + i, 1), :], pright[:, pl.ds(7 + i, 1), :])
        up, down = ue[:, i], ue[:, i + 2]
        out = apply_step(
            c[:fields], [x[:fields] for x in (up, down, low, high)],
            c[fields], [x[fields] for x in (up, down, low, high)], mix,
        )
        off = ((i == 0) & (lat == 0)) | ((i == tt + 1) & (lat == n_lat - 1))
        keep = jnp.where(off, 0.0, 1.0)
        for g in range(fields):
            first[g, i] = out[g] * keep
        return carry

    lax.fori_loop(0, tt + 2, first_row, 0)
    for side, outer, inner, into, ok in (
        (pleft, q2.at[0], sp.at[0], fleft, lon > 0),
        (pright, q2.at[1], sp.at[3], fright, lon < n_lon - 1),
    ):
        near = [side[:, 7 : 7 + tt, :], side[:, 9 : 9 + tt, :], outer[...], inner[...]]
        c = side[:, 8 : 8 + tt, :]
        out = apply_step(c[:fields], [x[:fields] for x in near], c[fields], [x[fields] for x in near], mix)
        keep = jnp.where(ok, 1.0, 0.0)
        for g in range(fields):
            into[g] = out[g] * keep

    other = lax.rem(me + 1, n_dev)
    all_dest = send_to(other, ds.at[0 : n_dev - 1], rd.at[0 : n_dev - 1], dest_send, dest_recv)
    all_vals = send_to(other, vs.at[0 : n_dev - 1], rv.at[0 : n_dev - 1], val_send, val_recv)
    all_dest.wait_recv()
    all_vals.wait_recv()

    face_p, face_t = helio.shape[1], helio.shape[2]
    acc[...] = jnp.zeros(acc.shape, F32)

    def land(i, carry):
        cell = jnp.concatenate([rd[i * LAND + k] for k in range(LAND)], axis=1).astype(jnp.int32) - 1
        val = jnp.concatenate([rv[i * LAND + k] for k in range(LAND)], axis=1)
        hi = val.astype(BF16).astype(F32)
        on_p = iota((face_p, LAND * LANES), 0) == (cell >> 7)
        on_t = jnp.where(iota((face_t, LAND * LANES), 0) == (cell & 127), 1.0, 0.0).astype(BF16)
        spread = jnp.concatenate(
            [jnp.where(on_p, x[f : f + 1], 0.0).astype(BF16) for x in (hi, val - hi) for f in range(fields)],
            axis=0,
        )
        acc[...] += dot_t(spread, on_t)
        return carry

    lax.fori_loop(0, n_dev // LAND, land, 0)
    half = fields * face_p
    flat = helio[...].reshape(half, face_t) + (acc[0:half] + acc[half:])
    coupled = flat.reshape(fields, face_p, face_t)

    for f in range(fields):
        hs[0, f : f + 1, :] = coupled[f, 0:1, :]
        hs[1, f : f + 1, :] = coupled[f, face_p - 1 : face_p, :]
    row8, lane8 = iota((8, face_t), 0), iota((8, face_t), 1)
    pick = jnp.where(
        ((row8 == 0) & (lane8 == 0)) | ((row8 == 1) & (lane8 == face_t - 1)), 1.0, 0.0
    )
    ts[...] = lax.dot_general(
        pick, flat, (((1,), (1,)), ((), ())), precision=lax.Precision.HIGHEST, preferred_element_type=F32
    )
    edges = [
        ((0, 1), hs.at[1], hr.at[0]),
        ((0, -1), hs.at[0], hr.at[1]),
        ((1, 0), ts, tr.at[0]),
        ((-1, 0), ts, tr.at[1]),
    ]
    launch(edges, face_send, face_recv)

    def second_row(t, carry):
        c = first[:, t + 1]
        low, high = shift_rows(c, fleft[:, pl.ds(t, 1), :], fright[:, pl.ds(t, 1), :])
        kc = ue[fields:, t + 2]
        klow, khigh = shift_rows(
            kc, pleft[fields:, pl.ds(8 + t, 1), :], pright[fields:, pl.ds(8 + t, 1), :]
        )
        out = apply_step(
            c, [first[:, t], first[:, t + 2], low, high],
            kc[0], [ue[fields, t + 1], ue[fields, t + 3], klow[0], khigh[0]], mix,
        )
        for g in range(fields):
            st[g, t] = out[g]
        return carry

    writes = []
    for h in range(2):
        part = slice(h * (tt // 2), (h + 1) * (tt // 2))
        lax.fori_loop(part.start, part.stop, second_row, 0)
        writes.append(pltpu.make_async_copy(st.at[:, part], stepped.at[:, part], out_sem.at[h]))
        writes[h].start()

    lane3 = iota(coupled.shape, 2)
    inner = (
        jnp.where(lane3 == 0, 0.0, pltpu.roll(coupled, 1, 2))
        + jnp.where(lane3 == face_t - 1, 0.0, pltpu.roll(coupled, face_t - 1, 2))
        - 4.0 * coupled
    )
    arrive(edges, face_send, face_recv)
    lows = jnp.concatenate([hr[0, f : f + 1, :][None] for f in range(fields)], axis=0)
    highs = jnp.concatenate([hr[1, f : f + 1, :][None] for f in range(fields)], axis=0)
    down, up = shift_rows(coupled, lows, highs)
    put_low = jnp.where((row8 == 1) & (lane8 == 0), 1.0, 0.0)
    put_high = jnp.where((row8 == 0) & (lane8 == face_t - 1), 1.0, 0.0)
    both = jnp.concatenate([tr[0], tr[1]], axis=0)
    sides = lax.dot_general(
        both, jnp.concatenate([put_low, put_high], axis=0), (((0,), (0,)), ((), ())),
        precision=lax.Precision.HIGHEST, preferred_element_type=F32,
    ).reshape(coupled.shape)
    face[...] = coupled + 0.2 * (inner + (down + up) + sides)
    write_face = pltpu.make_async_copy(face, face_out, face_sem)
    write_face.start()

    leave(small, small_send, small_recv)
    leave(moves, halo_send, halo_recv)
    leave(edges, face_send, face_recv)
    all_dest.wait_send()
    all_vals.wait_send()
    for copy in writes:
        copy.wait()
    write_face.wait()


def body(corona, kappa, mixing, helio_prev, owner, dest_cell, corner_base, fractions):
    n_lat, n_lon = lax.axis_size("lat"), lax.axis_size("lon")
    n_dev = n_lat * n_lon
    fields, tt, pp, n_r = corona.shape
    count = corner_base.shape[0]
    face_p, face_t = helio_prev.shape[1:]
    ext = fields + 1
    hbm = pl.BlockSpec(memory_space=pltpu.HBM)
    free = pl.BlockSpec(memory_space=pl.ANY)
    sem = pltpu.SemaphoreType.DMA
    v = lambda *shape: pltpu.VMEM(shape, F32)
    return pl.pallas_call(
        functools.partial(kernel, n_lat, n_lon),
        out_shape=(
            jax.ShapeDtypeStruct(corona.shape, F32),
            jax.ShapeDtypeStruct(helio_prev.shape, F32),
        ),
        in_specs=[hbm] * 8,
        out_specs=(free, free),
        scratch_shapes=[
            pltpu.SMEM(mixing.shape, F32),
            v(*mixing.shape),
            v(*helio_prev.shape),
            pltpu.VMEM((1, count), jnp.int32),
            pltpu.VMEM((1, count), jnp.int32),
            pltpu.VMEM((1, count), jnp.int32),
            v(3, count),
            v(*helio_prev.shape),
            v(tt + 4, fields, WIDE),
            v(tt + 4, 1, WIDE),
            v(tt + 2, fields, WIDE),
            v(tt + 2, fields, WIDE),
            v(tt, 7, 1, WIDE),
            v(ext, tt + 4, pp, n_r),
            v(4, ext, tt, n_r),
            v(ext, tt + 16, n_r),
            v(ext, tt + 16, n_r),
            v(2, ext, tt, n_r),
            v(4, 16, n_r),
            v(4, 16, n_r),
            v(fields, tt + 2, pp, n_r),
            v(fields, tt, n_r),
            v(fields, tt, n_r),
            v(fields, tt, pp, n_r),
            v(n_dev // GROUP, NPAR, GROUP, LANES),
            v(n_dev, 1, LANES),
            v(n_dev, 1, LANES),
            v(n_dev, fields, LANES),
            v(n_dev, fields, LANES),
            v(tt, fields, 2 * LANES),
            v(2, fields, face_t),
            v(2, fields, face_t),
            v(8, fields * face_p),
            v(2, 8, fields * face_p),
            v(2 * fields * face_p, face_t),
            sem((9,)), sem((10,)), sem((10,)), sem((16,)), sem((16,)), sem((2,)), sem,
            sem, sem, sem, sem, sem((4,)), sem((4,)),
        ],
        compiler_params=pltpu.CompilerParams(
            collective_id=0, has_side_effects=True, vmem_limit_bytes=63 * 1024 * 1024
        ),
        name="corona_helio",
    )(
        corona, kappa, mixing, helio_prev, owner.reshape(1, count), dest_cell.reshape(1, count),
        corner_base.reshape(1, count), fractions,
    )


def solution(mesh):
    return jax.shard_map(
        body,
        mesh=mesh,
        in_specs=(
            P(None, "lat", "lon", None),
            P("lat", "lon", None),
            P(),
            P(None, "lon", "lat"),
            P(("lat", "lon"), None),
            P(("lat", "lon")),
            P(("lat", "lon")),
            P(None, ("lat", "lon")),
        ),
        out_specs=(P(None, "lat", "lon", None), P(None, "lon", "lat")),
        check_vma=False,
    )
```

```python
import functools

import jax
import jax.numpy as jnp
from jax import lax
from jax.experimental import pallas as pl
from jax.experimental.pallas import tpu as pltpu
from jax.sharding import PartitionSpec as P

SH = 8
F32 = jnp.float32
BF16 = jnp.bfloat16
MESH = pl.DeviceIdType.MESH
LANES = 128
GROUP = 8
LAND = 4
NPAR = 5
DEEP = 16
WIDE = 4 * LANES


def iota(shape, dim):
    return lax.broadcasted_iota(jnp.int32, shape, dim)


def split(x):
    hi = x.astype(BF16)
    return hi, (x - hi.astype(F32)).astype(BF16)


def dot_t(a, b):
    return lax.dot_general(a, b, (((1,), (1,)), ((), ())), preferred_element_type=F32)


def apply_step(c, near, kc, knear, mix):
    lane = iota(kc.shape, 1)
    last = kc.shape[1] - 1
    ks = [0.075 * (kc + kn) for kn in knear]
    kl = 0.075 * (kc + jnp.where(lane == 0, 0.0, pltpu.roll(kc, 1, 1)))
    kr = 0.075 * (kc + jnp.where(lane == last, 0.0, pltpu.roll(kc, last, 1)))
    diag = 1.0 - (((ks[0] + ks[1]) + (ks[2] + ks[3])) + (kl + kr))
    kl = jnp.where(lane == 0, 0.0, kl)
    kr = jnp.where(lane == last, 0.0, kr)
    total = diag[None] * c
    for k, u in zip(ks, near):
        total = total + k[None] * u
    total = total + kl[None] * pltpu.roll(c, 1, 2) + kr[None] * pltpu.roll(c, last, 2)
    out = []
    for g in range(c.shape[0]):
        row = total[g]
        for f in range(c.shape[0]):
            row = row + (0.3 * mix[g, f]) * c[f]
        out.append(row)
    return out


def shift_rows(c, low, high):
    n = c.shape[1]
    row = iota(c.shape, 1)
    down = jnp.where(row == 0, low, pltpu.roll(c, 1, 1))
    up = jnp.where(row == n - 1, high, pltpu.roll(c, n - 1, 1))
    return down, up


def kernel(
    n_lat, n_lon, corona, kappa, mix_in, helio_in, owner_in, dest_in, base_in, frac_in, stepped, face_out,
    mix, mixv, helio, owner, dest, base, frac, face, xe, ke, xm, xf, co, ue, sp, pleft, pright, q2, cs, cr, first, fleft, fright, st, pk, ds, rd, vs, rv,
    shell, hs, hr, ts, tr, acc, load_sem, halo_send, halo_recv, small_send, small_recv, out_sem, face_sem,
    dest_send, dest_recv, val_send, val_recv, face_send, face_recv,
):
    n_dev = n_lat * n_lon
    fields = corona.shape[0]
    tt, pp = corona.shape[1], corona.shape[2]
    count = owner.shape[1]
    lat, lon = lax.axis_index("lat"), lax.axis_index("lon")
    me = lat * n_lon + lon

    loads = [
        pltpu.make_async_copy(corona, ue.at[0:fields, 2 : 2 + tt], load_sem.at[0]),
        pltpu.make_async_copy(kappa, ue.at[fields, 2 : 2 + tt], load_sem.at[1]),
    ] + [
        pltpu.make_async_copy(src, dst, load_sem.at[2 + k])
        for k, (src, dst) in enumerate(
            ((owner_in, owner), (base_in, base), (frac_in, frac), (dest_in, dest), (mix_in, mix), (mix_in, mixv), (helio_in, helio))
        )
    ]
    for copy in loads:
        copy.start()

    barrier = pltpu.get_barrier_semaphore()

    def greet(i, carry):
        o = lax.rem(me + i, n_dev)
        pl.semaphore_signal(
            barrier, inc=1, device_id=(lax.div(o, n_lon), lax.rem(o, n_lon)), device_id_type=MESH
        )
        return carry

    lax.fori_loop(1, n_dev, greet, 0)
    for copy in loads[:2]:
        copy.wait()

    per = LANES // DEEP
    lane1 = iota((1, LANES), 1)

    def extract(t, carry):
        lane = iota((fields, LANES), 1) // DEEP
        for h in range(pp // per):
            row = jnp.zeros((fields, LANES), F32)
            for j in range(per):
                x = pltpu.roll(ue[0:fields, t + 2, h * per + j, :], (j + 1) * DEEP % LANES, 1)
                row = jnp.where(lane == j, x, row)
            xe[t + 2, :, (h + 1) * LANES : (h + 2) * LANES] = row
        return carry

    lax.fori_loop(0, tt, extract, 0)
    lane_t = iota((tt, LANES), 1) // DEEP
    for h in range(pp // per):
        row = jnp.zeros((tt, LANES), F32)
        for j in range(per):
            x = pltpu.roll(ue[fields, 2 : 2 + tt, h * per + j, :], (j + 1) * DEEP % LANES, 1)
            row = jnp.where(lane_t == j, x, row)
        ke[2 : 2 + tt, :, (h + 1) * LANES : (h + 2) * LANES] = row[:, None, :]
    for ref in (xe, ke):
        for t in (0, tt + 3):
            for lo in (0, WIDE - LANES):
                ref[t, :, lo : lo + LANES] = jnp.zeros((ref.shape[1], LANES), F32)

    corners = [(1, 1), (1, -1), (-1, 1), (-1, -1)]
    moves = [
        ((1, 0), ue.at[:, tt : tt + 2], ue.at[:, 0:2]),
        ((-1, 0), ue.at[:, 2:4], ue.at[:, tt + 2 : tt + 4]),
        ((0, 1), sp.at[3], pleft.at[:, 8 : 8 + tt]),
        ((0, 1), sp.at[2], q2.at[0]),
        ((0, -1), sp.at[0], pright.at[:, 8 : 8 + tt]),
        ((0, -1), sp.at[1], q2.at[1]),
    ] + [(ab, cs.at[k], cr.at[k]) for k, ab in enumerate(corners)]

    mid = slice(LANES, WIDE - LANES)
    rows_in = slice(2, 2 + tt)
    places = [
        ((1, 0), (slice(tt, tt + 2), mid), (slice(0, 2), mid)),
        ((-1, 0), (slice(2, 4), mid), (slice(tt + 2, tt + 4), mid)),
        ((0, 1), (rows_in, slice(2 * LANES, 3 * LANES)), (rows_in, slice(0, LANES))),
        ((0, -1), (rows_in, slice(LANES, 2 * LANES)), (rows_in, slice(3 * LANES, WIDE))),
    ]
    for a, b in corners:
        src_t = slice(tt + 1, tt + 2) if a > 0 else slice(2, 3)
        dst_t = slice(1, 2) if a > 0 else slice(tt + 2, tt + 3)
        src_l = slice(2 * LANES, 3 * LANES) if b > 0 else slice(LANES, 2 * LANES)
        dst_l = slice(0, LANES) if b > 0 else slice(3 * LANES, WIDE)
        places.append(((a, b), (src_t, src_l), (dst_t, dst_l)))
    small = [
        (ab, ref.at[src[0], :, src[1]], ref.at[dst[0], :, dst[1]])
        for ab, src, dst in places
        for ref in (xe, ke)
    ]

    def inside(a, b):
        ok = lat >= 0
        if a > 0:
            ok = ok & (lat < n_lat - 1)
        if a < 0:
            ok = ok & (lat > 0)
        if b > 0:
            ok = ok & (lon < n_lon - 1)
        if b < 0:
            ok = ok & (lon > 0)
        return ok

    def remote(a, b, src, dst, send, recv):
        return pltpu.make_async_remote_copy(
            src_ref=src, dst_ref=dst, send_sem=send, recv_sem=recv,
            device_id=(lat + a, lon + b), device_id_type=MESH,
        )

    def launch(todo, send, recv):
        for k, ((a, b), src, dst) in enumerate(todo):

            @pl.when(inside(a, b))
            def _(k=k, a=a, b=b, src=src, dst=dst):
                remote(a, b, src, dst, send.at[k], recv.at[k]).start()

            @pl.when(jnp.logical_not(inside(-a, -b)))
            def _(dst=dst):
                dst[...] = jnp.zeros(dst.shape, F32)

    def arrive(todo, send, recv):
        for k, ((a, b), src, dst) in enumerate(todo):

            @pl.when(inside(-a, -b))
            def _(k=k, a=a, b=b, src=src, dst=dst):
                remote(-a, -b, src, dst, send.at[k], recv.at[k]).wait_recv()

    def leave(todo, send, recv):
        for k, ((a, b), src, dst) in enumerate(todo):

            @pl.when(inside(a, b))
            def _(k=k, a=a, b=b, src=src, dst=dst):
                remote(a, b, src, dst, send.at[k], recv.at[k]).wait_send()

    pl.semaphore_wait(barrier, n_dev - 1)
    launch(small, small_send, small_recv)
    for j, p in enumerate((0, 1, pp - 2, pp - 1)):
        sp[j] = ue[:, 2 : 2 + tt, p, :]
    for k, (a, b) in enumerate(corners):
        t, p = (2 + tt - 1 if a > 0 else 2), (pp - 1 if b > 0 else 0)
        for f in range(fields + 1):
            cs[k, f : f + 1, :] = ue[f, t, p : p + 1, :]

    launch(moves, halo_send, halo_recv)

    for copy in loads[2:]:
        copy.wait()

    own = owner[...]
    upper = (iota((LANES, LANES), 0) < iota((LANES, LANES), 1)).astype(F32).astype(BF16)
    carry = jnp.zeros((n_dev, 1), F32)
    ranks = []
    for blk in range(count // LANES):
        hit = jnp.where(
            iota((n_dev, LANES), 0) == own[:, blk * LANES : (blk + 1) * LANES], 1.0, 0.0
        )
        before = jnp.dot(hit.astype(BF16), upper, preferred_element_type=F32) + carry
        ranks.append(jnp.sum(hit * before, axis=0, keepdims=True))
        carry = carry + jnp.sum(hit, axis=1, keepdims=True)
    rank = jnp.concatenate(ranks, axis=1).astype(jnp.int32)
    rank_hot = jnp.where(iota((LANES, count), 0) == rank, 1.0, 0.0).astype(BF16)
    rows = [base[...].astype(F32)] + [frac[i : i + 1, :] for i in range(3)]
    rows.append((dest[...] + 1).astype(F32))
    pieces = []
    for row in rows:
        hi = row.astype(BF16).astype(F32)
        pieces += [hi, row - hi]
    chunk = 32

    def place(g, carry):
        mask = iota((chunk, count), 0) + g * chunk == own
        left = jnp.concatenate([jnp.where(mask, x, 0.0).astype(BF16) for x in pieces], axis=0)
        got = dot_t(left, rank_hot)
        for q in range(NPAR):
            val = got[2 * q * chunk : (2 * q + 1) * chunk] + got[(2 * q + 1) * chunk : (2 * q + 2) * chunk]
            for oc in range(chunk // GROUP):
                pk[g * (chunk // GROUP) + oc, q] = val[oc * GROUP : (oc + 1) * GROUP]
            if q == NPAR - 1:
                for o in range(chunk):
                    ds[g * chunk + o] = val[o : o + 1]
        return carry

    lax.fori_loop(0, n_dev // chunk, place, 0)

    def send_to(o, src, dst, send, recv):
        return pltpu.make_async_remote_copy(
            src_ref=src, dst_ref=dst, send_sem=send, recv_sem=recv,
            device_id=(lax.div(o, n_lon), lax.rem(o, n_lon)), device_id_type=MESH,
        )

    def send_dest(i, carry):
        o = lax.rem(me + i, n_dev)
        send_to(o, ds.at[o], rd.at[me], dest_send, dest_recv).start()
        return carry

    lax.fori_loop(1, n_dev, send_dest, 0)
    rd[me] = ds[me]

    nrow = (tt + 2) * fields
    hot = jnp.where(iota((nrow, fields), 0) % fields == iota((nrow, fields), 1), 1.0, 0.0)
    wide_mix = lax.dot_general(
        jnp.dot(hot, 0.3 * mixv[...], precision=lax.Precision.HIGHEST, preferred_element_type=F32),
        hot, (((1,), (1,)), ((), ())), precision=lax.Precision.HIGHEST, preferred_element_type=F32,
    )
    same = iota((nrow, nrow), 0) // fields == iota((nrow, nrow), 1) // fields
    m_hi, m_lo = split(jnp.where(same, wide_mix, 0.0))

    def mixed(x, n):
        hi, lo = split(x)
        mh, ml = m_hi[:n, :n], m_lo[:n, :n]
        dot = lambda a, b: jnp.dot(a, b, preferred_element_type=F32)
        return dot(mh, hi) + (dot(mh, lo) + dot(ml, hi))

    arrive(small, small_send, small_recv)
    xm[...] = mixed(xe[1 : tt + 3].reshape(nrow, WIDE), nrow).reshape(tt + 2, fields, WIDE)
    lane = iota((1, WIDE), 1)
    top = lane % DEEP == DEEP - 1
    outside = ((lane < LANES) & (lon == 0)) | ((lane >= WIDE - LANES) & (lon == n_lon - 1))
    keep_lane = jnp.where(outside, 0.0, 1.0)

    def roll(x, by):
        return pltpu.roll(x, by % WIDE, 1)

    def compact_row(c, up, down, k, more):
        return (
            more + k[6] * c + (k[0] * up + k[1] * down) + (k[2] * roll(c, DEEP) + k[3] * roll(c, -DEEP))
            + (k[4] * roll(c, 1) + k[5] * roll(c, -1))
        )

    def compact_first(i, carry):
        kc = ke[i + 1]
        k = [0.075 * (kc + x) for x in (ke[i], ke[i + 2], roll(kc, DEEP), roll(kc, -DEEP), roll(kc, 1))]
        outer = 0.075 * (kc + jnp.where(top, 0.0, roll(kc, -1)))
        diag = 1.0 - (((k[0] + k[1]) + (k[2] + k[3])) + (k[4] + outer))
        k += [jnp.where(top, 0.0, outer), diag]
        off = ((i == 0) & (lat == 0)) | ((i == tt + 1) & (lat == n_lat - 1))
        keep = keep_lane * jnp.where(off, 0.0, 1.0)
        xf[i] = keep * compact_row(xe[i + 1], xe[i], xe[i + 2], k, xm[i])

        @pl.when((i > 0) & (i < tt + 1))
        def _():
            for q in range(7):
                co[i - 1, q] = k[q]

        return carry

    lax.fori_loop(0, tt + 2, compact_first, 0)
    xm[0:tt] = mixed(xf[1 : tt + 1].reshape(tt * fields, WIDE), tt * fields).reshape(tt, fields, WIDE)

    def compact_second(t, carry):
        out = compact_row(xf[t + 1], xf[t], xf[t + 2], [co[t, q] for q in range(7)], xm[t])
        shell[t] = out[:, mid]
        return carry

    lax.fori_loop(0, tt, compact_second, 0)
    deep_at, cell_at = iota((2 * LANES, LANES), 0), iota((2 * LANES, LANES), 1)
    take = jnp.where(
        (deep_at // DEEP == cell_at // SH) & (deep_at % DEEP == cell_at % SH + DEEP - SH), 1.0, 0.0
    ).astype(BF16)
    s_hi, s_lo = [
        jnp.dot(x, take, preferred_element_type=F32).astype(BF16)
        for x in split(shell[...].reshape(tt * fields, 2 * LANES))
    ]
    left = jnp.concatenate([s_hi, s_hi, s_lo], axis=1)
    groups = n_dev // GROUP
    wide = GROUP * LANES

    def values(i, carry):
        g = lax.rem(lax.div(me, GROUP) + i, groups)
        par = [
            jnp.concatenate([pk[g, q, k : k + 1, :] for k in range(GROUP)], axis=1)
            for q in range(NPAR - 1)
        ]
        cell = par[0].astype(jnp.int32)
        t0, p0, r0 = cell >> 7, (cell >> 3) & 15, cell & 7
        fx, fy, fz = par[1:]

        def weights(n, at, fr):
            idx = iota((n, wide), 0) - at
            return jnp.where(idx == 0, 1.0 - fr, jnp.where(idx == 1, fr, 0.0))

        wa, wb, wc = weights(tt, t0, fx), weights(pp, p0, fy), weights(SH, r0, fz)
        table = (wb[:, None, :] * wc[None]).reshape(pp * SH, wide)
        hi, lo = split(table)
        got = jnp.dot(left, jnp.concatenate([hi, lo, hi], axis=0), preferred_element_type=F32)
        val = jnp.sum(got.reshape(tt, fields, wide) * wa[:, None, :], axis=0)
        for k in range(GROUP):
            vs[g * GROUP + k] = val[:, k * LANES : (k + 1) * LANES]
        for k in range(GROUP):
            o = g * GROUP + k

            @pl.when(o != me)
            def _(o=o):
                send_to(o, vs.at[o], rv.at[me], val_send, val_recv).start()

        return carry

    lax.fori_loop(0, groups, values, 0)
    rv[me] = vs[me]

    arrive(moves, halo_send, halo_recv)
    for k, (a, b) in enumerate(corners):
        side = pleft if b > 0 else pright
        row = 7 if a > 0 else 8 + tt
        for f in range(fields + 1):
            side[f, row : row + 1, :] = cr[k, f : f + 1, :]

    def first_row(i, carry):
        c = ue[:, i + 1]
        low, high = shift_rows(c, pleft[:, pl.ds(7 + i, 1), :], pright[:, pl.ds(7 + i, 1), :])
        up, down = ue[:, i], ue[:, i + 2]
        out = apply_step(
            c[:fields], [x[:fields] for x in (up, down, low, high)],
            c[fields], [x[fields] for x in (up, down, low, high)], mix,
        )
        off = ((i == 0) & (lat == 0)) | ((i == tt + 1) & (lat == n_lat - 1))
        keep = jnp.where(off, 0.0, 1.0)
        for g in range(fields):
            first[g, i] = out[g] * keep
        return carry

    lax.fori_loop(0, tt + 2, first_row, 0)
    for side, outer, inner, into, ok in (
        (pleft, q2.at[0], sp.at[0], fleft, lon > 0),
        (pright, q2.at[1], sp.at[3], fright, lon < n_lon - 1),
    ):
        near = [side[:, 7 : 7 + tt, :], side[:, 9 : 9 + tt, :], outer[...], inner[...]]
        c = side[:, 8 : 8 + tt, :]
        out = apply_step(c[:fields], [x[:fields] for x in near], c[fields], [x[fields] for x in near], mix)
        keep = jnp.where(ok, 1.0, 0.0)
        for g in range(fields):
            into[g] = out[g] * keep

    other = lax.rem(me + 1, n_dev)
    all_dest = send_to(other, ds.at[0 : n_dev - 1], rd.at[0 : n_dev - 1], dest_send, dest_recv)
    all_vals = send_to(other, vs.at[0 : n_dev - 1], rv.at[0 : n_dev - 1], val_send, val_recv)
    all_dest.wait_recv()
    all_vals.wait_recv()

    face_p, face_t = helio.shape[1], helio.shape[2]
    acc[...] = jnp.zeros(acc.shape, F32)

    def land(i, carry):
        cell = jnp.concatenate([rd[i * LAND + k] for k in range(LAND)], axis=1).astype(jnp.int32) - 1
        val = jnp.concatenate([rv[i * LAND + k] for k in range(LAND)], axis=1)
        hi = val.astype(BF16).astype(F32)
        on_p = iota((face_p, LAND * LANES), 0) == (cell >> 7)
        on_t = jnp.where(iota((face_t, LAND * LANES), 0) == (cell & 127), 1.0, 0.0).astype(BF16)
        spread = jnp.concatenate(
            [jnp.where(on_p, x[f : f + 1], 0.0).astype(BF16) for x in (hi, val - hi) for f in range(fields)],
            axis=0,
        )
        acc[...] += dot_t(spread, on_t)
        return carry

    lax.fori_loop(0, n_dev // LAND, land, 0)
    half = fields * face_p
    flat = helio[...].reshape(half, face_t) + (acc[0:half] + acc[half:])
    coupled = flat.reshape(fields, face_p, face_t)

    for f in range(fields):
        hs[0, f : f + 1, :] = coupled[f, 0:1, :]
        hs[1, f : f + 1, :] = coupled[f, face_p - 1 : face_p, :]
    row8, lane8 = iota((8, face_t), 0), iota((8, face_t), 1)
    pick = jnp.where(
        ((row8 == 0) & (lane8 == 0)) | ((row8 == 1) & (lane8 == face_t - 1)), 1.0, 0.0
    )
    ts[...] = lax.dot_general(
        pick, flat, (((1,), (1,)), ((), ())), precision=lax.Precision.HIGHEST, preferred_element_type=F32
    )
    edges = [
        ((0, 1), hs.at[1], hr.at[0]),
        ((0, -1), hs.at[0], hr.at[1]),
        ((1, 0), ts, tr.at[0]),
        ((-1, 0), ts, tr.at[1]),
    ]
    launch(edges, face_send, face_recv)

    def second_row(t, carry):
        c = first[:, t + 1]
        low, high = shift_rows(c, fleft[:, pl.ds(t, 1), :], fright[:, pl.ds(t, 1), :])
        kc = ue[fields:, t + 2]
        klow, khigh = shift_rows(
            kc, pleft[fields:, pl.ds(8 + t, 1), :], pright[fields:, pl.ds(8 + t, 1), :]
        )
        out = apply_step(
            c, [first[:, t], first[:, t + 2], low, high],
            kc[0], [ue[fields, t + 1], ue[fields, t + 3], klow[0], khigh[0]], mix,
        )
        for g in range(fields):
            st[g, t] = out[g]
        return carry

    writes = []
    for h in range(2):
        part = slice(h * (tt // 2), (h + 1) * (tt // 2))
        lax.fori_loop(part.start, part.stop, second_row, 0)
        writes.append(pltpu.make_async_copy(st.at[:, part], stepped.at[:, part], out_sem.at[h]))
        writes[h].start()

    lane3 = iota(coupled.shape, 2)
    inner = (
        jnp.where(lane3 == 0, 0.0, pltpu.roll(coupled, 1, 2))
        + jnp.where(lane3 == face_t - 1, 0.0, pltpu.roll(coupled, face_t - 1, 2))
        - 4.0 * coupled
    )
    arrive(edges, face_send, face_recv)
    lows = jnp.concatenate([hr[0, f : f + 1, :][None] for f in range(fields)], axis=0)
    highs = jnp.concatenate([hr[1, f : f + 1, :][None] for f in range(fields)], axis=0)
    down, up = shift_rows(coupled, lows, highs)
    put_low = jnp.where((row8 == 1) & (lane8 == 0), 1.0, 0.0)
    put_high = jnp.where((row8 == 0) & (lane8 == face_t - 1), 1.0, 0.0)
    both = jnp.concatenate([tr[0], tr[1]], axis=0)
    sides = lax.dot_general(
        both, jnp.concatenate([put_low, put_high], axis=0), (((0,), (0,)), ((), ())),
        precision=lax.Precision.HIGHEST, preferred_element_type=F32,
    ).reshape(coupled.shape)
    face[...] = coupled + 0.2 * (inner + (down + up) + sides)
    write_face = pltpu.make_async_copy(face, face_out, face_sem)
    write_face.start()

    leave(small, small_send, small_recv)
    leave(moves, halo_send, halo_recv)
    leave(edges, face_send, face_recv)
    all_dest.wait_send()
    all_vals.wait_send()
    for copy in writes:
        copy.wait()
    write_face.wait()


def body(corona, kappa, mixing, helio_prev, owner, dest_cell, corner_base, fractions):
    n_lat, n_lon = lax.axis_size("lat"), lax.axis_size("lon")
    n_dev = n_lat * n_lon
    fields, tt, pp, n_r = corona.shape
    count = corner_base.shape[0]
    face_p, face_t = helio_prev.shape[1:]
    ext = fields + 1
    hbm = pl.BlockSpec(memory_space=pltpu.HBM)
    free = pl.BlockSpec(memory_space=pl.ANY)
    sem = pltpu.SemaphoreType.DMA
    v = lambda *shape: pltpu.VMEM(shape, F32)
    return pl.pallas_call(
        functools.partial(kernel, n_lat, n_lon),
        out_shape=(
            jax.ShapeDtypeStruct(corona.shape, F32),
            jax.ShapeDtypeStruct(helio_prev.shape, F32),
        ),
        in_specs=[hbm] * 8,
        out_specs=(free, free),
        scratch_shapes=[
            pltpu.SMEM(mixing.shape, F32),
            v(*mixing.shape),
            v(*helio_prev.shape),
            pltpu.VMEM((1, count), jnp.int32),
            pltpu.VMEM((1, count), jnp.int32),
            pltpu.VMEM((1, count), jnp.int32),
            v(3, count),
            v(*helio_prev.shape),
            v(tt + 4, fields, WIDE),
            v(tt + 4, 1, WIDE),
            v(tt + 2, fields, WIDE),
            v(tt + 2, fields, WIDE),
            v(tt, 7, 1, WIDE),
            v(ext, tt + 4, pp, n_r),
            v(4, ext, tt, n_r),
            v(ext, tt + 16, n_r),
            v(ext, tt + 16, n_r),
            v(2, ext, tt, n_r),
            v(4, 16, n_r),
            v(4, 16, n_r),
            v(fields, tt + 2, pp, n_r),
            v(fields, tt, n_r),
            v(fields, tt, n_r),
            v(fields, tt, pp, n_r),
            v(n_dev // GROUP, NPAR, GROUP, LANES),
            v(n_dev, 1, LANES),
            v(n_dev, 1, LANES),
            v(n_dev, fields, LANES),
            v(n_dev, fields, LANES),
            v(tt, fields, 2 * LANES),
            v(2, fields, face_t),
            v(2, fields, face_t),
            v(8, fields * face_p),
            v(2, 8, fields * face_p),
            v(2 * fields * face_p, face_t),
            sem((9,)), sem((10,)), sem((10,)), sem((16,)), sem((16,)), sem((2,)), sem,
            sem, sem, sem, sem, sem((4,)), sem((4,)),
        ],
        compiler_params=pltpu.CompilerParams(
            collective_id=0, has_side_effects=True, vmem_limit_bytes=48 * 1024 * 1024
        ),
        name="corona_helio",
    )(
        *[
            pltpu.with_memory_space_constraint(x, pltpu.HBM)
            for x in (
                corona, kappa, mixing, helio_prev, owner.reshape(1, count), dest_cell.reshape(1, count),
                corner_base.reshape(1, count), fractions,
            )
        ]
    )


def solution(mesh):
    return jax.shard_map(
        body,
        mesh=mesh,
        in_specs=(
            P(None, "lat", "lon", None),
            P("lat", "lon", None),
            P(),
            P(None, "lon", "lat"),
            P(("lat", "lon"), None),
            P(("lat", "lon")),
            P(("lat", "lon")),
            P(None, ("lat", "lon")),
        ),
        out_specs=(P(None, "lat", "lon", None), P(None, "lon", "lat")),
        check_vma=False,
    )
```

```python
import functools

import jax
import jax.numpy as jnp
from jax import lax
from jax.experimental import pallas as pl
from jax.experimental.pallas import tpu as pltpu
from jax.sharding import PartitionSpec as P

SH = 8
F32 = jnp.float32
BF16 = jnp.bfloat16
MESH = pl.DeviceIdType.MESH
LANES = 128
GROUP = 8
LAND = 4
NPAR = 5
DEEP = 16
WIDE = 4 * LANES


def iota(shape, dim):
    return lax.broadcasted_iota(jnp.int32, shape, dim)


def split(x):
    hi = x.astype(BF16)
    return hi, (x - hi.astype(F32)).astype(BF16)


def dot_t(a, b):
    return lax.dot_general(a, b, (((1,), (1,)), ((), ())), preferred_element_type=F32)


def apply_step(c, near, kc, knear, mb):
    lane = iota(kc.shape, 1)
    last = kc.shape[1] - 1
    ks = [0.075 * (kc + kn) for kn in knear]
    kl = 0.075 * (kc + jnp.where(lane == 0, 0.0, pltpu.roll(kc, 1, 1)))
    kr = 0.075 * (kc + jnp.where(lane == last, 0.0, pltpu.roll(kc, last, 1)))
    diag = 1.0 - (((ks[0] + ks[1]) + (ks[2] + ks[3])) + (kl + kr))
    kl = jnp.where(lane == 0, 0.0, kl)
    kr = jnp.where(lane == last, 0.0, kr)
    total = diag[None] * c
    for k, u in zip(ks, near):
        total = total + k[None] * u
    total = total + kl[None] * pltpu.roll(c, 1, 2) + kr[None] * pltpu.roll(c, last, 2)
    tiles = (c.shape[1] // 8, 8, c.shape[2])
    total = total.reshape((c.shape[0],) + tiles)
    for f in range(c.shape[0]):
        total = total + mb[f][:, None] * c[f].reshape(tiles)[None]
    return total.reshape(c.shape)


def shift_rows(c, low, high):
    n = c.shape[1]
    row = iota(c.shape, 1)
    down = jnp.where(row == 0, low, pltpu.roll(c, 1, 1))
    up = jnp.where(row == n - 1, high, pltpu.roll(c, n - 1, 1))
    return down, up


def kernel(
    n_lat, n_lon, corona, kappa, mix_in, helio_in, owner_in, dest_in, base_in, frac_in, stepped, face_out,
    mix, mixv, mb, helio, owner, dest, base, frac, face, xe, ke, xm, xf, co, ue, sp, pleft, pright, q2, cs, cr, first, fleft, fright, st, pk, ds, rd, vs, rv,
    shell, hs, hr, ts, tr, acc, load_sem, halo_send, halo_recv, small_send, small_recv, out_sem, face_sem,
    dest_send, dest_recv, val_send, val_recv, face_send, face_recv,
):
    n_dev = n_lat * n_lon
    fields = corona.shape[0]
    tt, pp = corona.shape[1], corona.shape[2]
    count = owner.shape[1]
    lat, lon = lax.axis_index("lat"), lax.axis_index("lon")
    me = lat * n_lon + lon

    loads = [
        pltpu.make_async_copy(corona, ue.at[0:fields, 2 : 2 + tt], load_sem.at[0]),
        pltpu.make_async_copy(kappa, ue.at[fields, 2 : 2 + tt], load_sem.at[1]),
    ] + [
        pltpu.make_async_copy(src, dst, load_sem.at[2 + k])
        for k, (src, dst) in enumerate(
            ((owner_in, owner), (base_in, base), (frac_in, frac), (dest_in, dest), (mix_in, mix), (mix_in, mixv), (helio_in, helio))
        )
    ]
    for copy in loads:
        copy.start()

    barrier = pltpu.get_barrier_semaphore()

    def greet(i, carry):
        o = lax.rem(me + i, n_dev)
        pl.semaphore_signal(
            barrier, inc=1, device_id=(lax.div(o, n_lon), lax.rem(o, n_lon)), device_id_type=MESH
        )
        return carry

    lax.fori_loop(1, n_dev, greet, 0)
    for copy in loads[:2]:
        copy.wait()

    per = LANES // DEEP
    lane1 = iota((1, LANES), 1)

    def extract(i, carry):
        lane = iota((fields, LANES), 1) // DEEP
        for t in [4 * i + k for k in range(4)]:
            for h in range(pp // per):
                row = jnp.zeros((fields, LANES), F32)
                for j in range(per):
                    x = pltpu.roll(ue[0:fields, t + 2, h * per + j, :], (j + 1) * DEEP % LANES, 1)
                    row = jnp.where(lane == j, x, row)
                xe[t + 2, :, (h + 1) * LANES : (h + 2) * LANES] = row
        return carry

    lax.fori_loop(0, tt // 4, extract, 0)
    lane_t = iota((tt, LANES), 1) // DEEP
    for h in range(pp // per):
        row = jnp.zeros((tt, LANES), F32)
        for j in range(per):
            x = pltpu.roll(ue[fields, 2 : 2 + tt, h * per + j, :], (j + 1) * DEEP % LANES, 1)
            row = jnp.where(lane_t == j, x, row)
        ke[2 : 2 + tt, :, (h + 1) * LANES : (h + 2) * LANES] = row[:, None, :]
    for ref in (xe, ke):
        for t in (0, tt + 3):
            for lo in (0, WIDE - LANES):
                ref[t, :, lo : lo + LANES] = jnp.zeros((ref.shape[1], LANES), F32)

    corners = [(1, 1), (1, -1), (-1, 1), (-1, -1)]
    moves = [
        ((1, 0), ue.at[:, tt : tt + 2], ue.at[:, 0:2]),
        ((-1, 0), ue.at[:, 2:4], ue.at[:, tt + 2 : tt + 4]),
        ((0, 1), sp.at[3], pleft.at[:, 8 : 8 + tt]),
        ((0, 1), sp.at[2], q2.at[0]),
        ((0, -1), sp.at[0], pright.at[:, 8 : 8 + tt]),
        ((0, -1), sp.at[1], q2.at[1]),
    ] + [(ab, cs.at[k], cr.at[k]) for k, ab in enumerate(corners)]

    mid = slice(LANES, WIDE - LANES)
    rows_in = slice(2, 2 + tt)
    places = [
        ((1, 0), (slice(tt, tt + 2), mid), (slice(0, 2), mid)),
        ((-1, 0), (slice(2, 4), mid), (slice(tt + 2, tt + 4), mid)),
        ((0, 1), (rows_in, slice(2 * LANES, 3 * LANES)), (rows_in, slice(0, LANES))),
        ((0, -1), (rows_in, slice(LANES, 2 * LANES)), (rows_in, slice(3 * LANES, WIDE))),
    ]
    for a, b in corners:
        src_t = slice(tt + 1, tt + 2) if a > 0 else slice(2, 3)
        dst_t = slice(1, 2) if a > 0 else slice(tt + 2, tt + 3)
        src_l = slice(2 * LANES, 3 * LANES) if b > 0 else slice(LANES, 2 * LANES)
        dst_l = slice(0, LANES) if b > 0 else slice(3 * LANES, WIDE)
        places.append(((a, b), (src_t, src_l), (dst_t, dst_l)))
    small = [
        (ab, ref.at[src[0], :, src[1]], ref.at[dst[0], :, dst[1]])
        for ab, src, dst in places
        for ref in (xe, ke)
    ]

    def inside(a, b):
        ok = lat >= 0
        if a > 0:
            ok = ok & (lat < n_lat - 1)
        if a < 0:
            ok = ok & (lat > 0)
        if b > 0:
            ok = ok & (lon < n_lon - 1)
        if b < 0:
            ok = ok & (lon > 0)
        return ok

    def remote(a, b, src, dst, send, recv):
        return pltpu.make_async_remote_copy(
            src_ref=src, dst_ref=dst, send_sem=send, recv_sem=recv,
            device_id=(lat + a, lon + b), device_id_type=MESH,
        )

    def launch(todo, send, recv):
        for k, ((a, b), src, dst) in enumerate(todo):

            @pl.when(inside(a, b))
            def _(k=k, a=a, b=b, src=src, dst=dst):
                remote(a, b, src, dst, send.at[k], recv.at[k]).start()

            @pl.when(jnp.logical_not(inside(-a, -b)))
            def _(dst=dst):
                dst[...] = jnp.zeros(dst.shape, F32)

    def arrive(todo, send, recv):
        for k, ((a, b), src, dst) in enumerate(todo):

            @pl.when(inside(-a, -b))
            def _(k=k, a=a, b=b, src=src, dst=dst):
                remote(-a, -b, src, dst, send.at[k], recv.at[k]).wait_recv()

    def leave(todo, send, recv):
        for k, ((a, b), src, dst) in enumerate(todo):

            @pl.when(inside(a, b))
            def _(k=k, a=a, b=b, src=src, dst=dst):
                remote(a, b, src, dst, send.at[k], recv.at[k]).wait_send()

    pl.semaphore_wait(barrier, n_dev - 1)
    launch(small, small_send, small_recv)
    for j, p in enumerate((0, 1, pp - 2, pp - 1)):
        sp[j] = ue[:, 2 : 2 + tt, p, :]
    for k, (a, b) in enumerate(corners):
        t, p = (2 + tt - 1 if a > 0 else 2), (pp - 1 if b > 0 else 0)
        for f in range(fields + 1):
            cs[k, f : f + 1, :] = ue[f, t, p : p + 1, :]

    launch(moves, halo_send, halo_recv)

    for copy in loads[2:]:
        copy.wait()

    for f in range(fields):
        for g in range(fields):
            mb[f, g] = jnp.full((8, LANES), 0.3 * mix[g, f], F32)

    own = owner[...]
    upper = (iota((LANES, LANES), 0) < iota((LANES, LANES), 1)).astype(F32).astype(BF16)
    carry = jnp.zeros((n_dev, 1), F32)
    ranks = []
    for blk in range(count // LANES):
        hit = jnp.where(
            iota((n_dev, LANES), 0) == own[:, blk * LANES : (blk + 1) * LANES], 1.0, 0.0
        )
        before = jnp.dot(hit.astype(BF16), upper, preferred_element_type=F32) + carry
        ranks.append(jnp.sum(hit * before, axis=0, keepdims=True))
        carry = carry + jnp.sum(hit, axis=1, keepdims=True)
    rank = jnp.concatenate(ranks, axis=1).astype(jnp.int32)
    rank_hot = jnp.where(iota((LANES, count), 0) == rank, 1.0, 0.0).astype(BF16)
    rows = [base[...].astype(F32)] + [frac[i : i + 1, :] for i in range(3)]
    rows.append((dest[...] + 1).astype(F32))
    pieces = []
    for row in rows:
        hi = row.astype(BF16).astype(F32)
        pieces += [hi, row - hi]
    chunk = 32

    def place(g, carry):
        mask = iota((chunk, count), 0) + g * chunk == own
        left = jnp.concatenate([jnp.where(mask, x, 0.0).astype(BF16) for x in pieces], axis=0)
        got = dot_t(left, rank_hot)
        for q in range(NPAR):
            val = got[2 * q * chunk : (2 * q + 1) * chunk] + got[(2 * q + 1) * chunk : (2 * q + 2) * chunk]
            for oc in range(chunk // GROUP):
                pk[g * (chunk // GROUP) + oc, q] = val[oc * GROUP : (oc + 1) * GROUP]
            if q == NPAR - 1:
                for o in range(chunk):
                    ds[g * chunk + o] = val[o : o + 1]
        return carry

    lax.fori_loop(0, n_dev // chunk, place, 0)

    def send_to(o, src, dst, send, recv):
        return pltpu.make_async_remote_copy(
            src_ref=src, dst_ref=dst, send_sem=send, recv_sem=recv,
            device_id=(lax.div(o, n_lon), lax.rem(o, n_lon)), device_id_type=MESH,
        )

    def send_dest(i, carry):
        o = lax.rem(me + i, n_dev)
        send_to(o, ds.at[o], rd.at[me], dest_send, dest_recv).start()
        return carry

    lax.fori_loop(1, n_dev, send_dest, 0)
    rd[me] = ds[me]

    nrow = (tt + 2) * fields
    hot = jnp.where(iota((nrow, fields), 0) % fields == iota((nrow, fields), 1), 1.0, 0.0)
    wide_mix = lax.dot_general(
        jnp.dot(hot, 0.3 * mixv[...], precision=lax.Precision.HIGHEST, preferred_element_type=F32),
        hot, (((1,), (1,)), ((), ())), precision=lax.Precision.HIGHEST, preferred_element_type=F32,
    )
    same = iota((nrow, nrow), 0) // fields == iota((nrow, nrow), 1) // fields
    m_hi, m_lo = split(jnp.where(same, wide_mix, 0.0))

    def mixed(x, n):
        hi, lo = split(x)
        mh, ml = m_hi[:n, :n], m_lo[:n, :n]
        dot = lambda a, b: jnp.dot(a, b, preferred_element_type=F32)
        return dot(mh, hi) + (dot(mh, lo) + dot(ml, hi))

    arrive(small, small_send, small_recv)
    xm[...] = mixed(xe[1 : tt + 3].reshape(nrow, WIDE), nrow).reshape(tt + 2, fields, WIDE)
    lane = iota((1, 1, WIDE), 2)
    top = lane % DEEP == DEEP - 1
    outside = ((lane < LANES) & (lon == 0)) | ((lane >= WIDE - LANES) & (lon == n_lon - 1))
    keep_lane = jnp.where(outside, 0.0, 1.0)

    def roll(x, by):
        return pltpu.roll(x, by % WIDE, 2)

    def compact_rows(c, up, down, k, more):
        return (
            more + k[6] * c + (k[0] * up + k[1] * down) + (k[2] * roll(c, DEEP) + k[3] * roll(c, -DEEP))
            + (k[4] * roll(c, 1) + k[5] * roll(c, -1))
        )

    def compact_first(j, carry):
        n = 6
        i = j * n
        at = lambda ref, d: ref[pl.ds(i + d, n)]
        kc = at(ke, 1)
        k = [0.075 * (kc + x) for x in (at(ke, 0), at(ke, 2), roll(kc, DEEP), roll(kc, -DEEP), roll(kc, 1))]
        outer = 0.075 * (kc + jnp.where(top, 0.0, roll(kc, -1)))
        diag = 1.0 - (((k[0] + k[1]) + (k[2] + k[3])) + (k[4] + outer))
        k += [jnp.where(top, 0.0, outer), diag]
        row = iota((n, 1, WIDE), 0) + i
        off = ((row == 0) & (lat == 0)) | ((row == tt + 1) & (lat == n_lat - 1))
        keep = jnp.where(off, 0.0, keep_lane)
        xf[pl.ds(i, n)] = keep * compact_rows(at(xe, 1), at(xe, 0), at(xe, 2), k, at(xm, 0))
        for q in range(7):
            co[q, pl.ds(i, n)] = k[q]
        return carry

    lax.fori_loop(0, (tt + 2) // 6, compact_first, 0)
    xm[0:tt] = mixed(xf[1 : tt + 1].reshape(tt * fields, WIDE), tt * fields).reshape(tt, fields, WIDE)

    def compact_second(j, carry):
        n = 4
        t = j * n
        at = lambda ref, d: ref[pl.ds(t + d, n)]
        k = [co[q, pl.ds(t + 1, n)] for q in range(7)]
        out = compact_rows(at(xf, 1), at(xf, 0), at(xf, 2), k, at(xm, 0))
        shell[pl.ds(t, n)] = out[:, :, mid]
        return carry

    lax.fori_loop(0, tt // 4, compact_second, 0)
    deep_at, cell_at = iota((2 * LANES, LANES), 0), iota((2 * LANES, LANES), 1)
    take = jnp.where(
        (deep_at // DEEP == cell_at // SH) & (deep_at % DEEP == cell_at % SH + DEEP - SH), 1.0, 0.0
    ).astype(BF16)
    s_hi, s_lo = [
        jnp.dot(x, take, preferred_element_type=F32).astype(BF16)
        for x in split(shell[...].reshape(tt * fields, 2 * LANES))
    ]
    left = jnp.concatenate([s_hi, s_hi, s_lo], axis=1)
    groups = n_dev // GROUP
    wide = GROUP * LANES

    def values(i, carry):
        g = lax.rem(lax.div(me, GROUP) + i, groups)
        par = [
            jnp.concatenate([pk[g, q, k : k + 1, :] for k in range(GROUP)], axis=1)
            for q in range(NPAR - 1)
        ]
        cell = par[0].astype(jnp.int32)
        t0, p0, r0 = cell >> 7, (cell >> 3) & 15, cell & 7
        fx, fy, fz = par[1:]

        def weights(n, at, fr):
            idx = iota((n, wide), 0) - at
            return jnp.where(idx == 0, 1.0 - fr, jnp.where(idx == 1, fr, 0.0))

        wa, wb, wc = weights(tt, t0, fx), weights(pp, p0, fy), weights(SH, r0, fz)
        table = (wb[:, None, :] * wc[None]).reshape(pp * SH, wide)
        hi, lo = split(table)
        got = jnp.dot(left, jnp.concatenate([hi, lo, hi], axis=0), preferred_element_type=F32)
        val = jnp.sum(got.reshape(tt, fields, wide) * wa[:, None, :], axis=0)
        for k in range(GROUP):
            vs[g * GROUP + k] = val[:, k * LANES : (k + 1) * LANES]
        for k in range(GROUP):
            o = g * GROUP + k

            @pl.when(o != me)
            def _(o=o):
                send_to(o, vs.at[o], rv.at[me], val_send, val_recv).start()

        return carry

    lax.fori_loop(0, groups, values, 0)
    rv[me] = vs[me]

    arrive(moves, halo_send, halo_recv)
    for k, (a, b) in enumerate(corners):
        side = pleft if b > 0 else pright
        row = 7 if a > 0 else 8 + tt
        for f in range(fields + 1):
            side[f, row : row + 1, :] = cr[k, f : f + 1, :]

    def first_row(i):
        c = ue[:, i + 1]
        low, high = shift_rows(c, pleft[:, pl.ds(7 + i, 1), :], pright[:, pl.ds(7 + i, 1), :])
        up, down = ue[:, i], ue[:, i + 2]
        out = apply_step(
            c[:fields], [x[:fields] for x in (up, down, low, high)],
            c[fields], [x[fields] for x in (up, down, low, high)], mb,
        )
        off = ((i == 0) & (lat == 0)) | ((i == tt + 1) & (lat == n_lat - 1))
        keep = jnp.where(off, 0.0, 1.0)
        first[:, i] = out * keep

    def first_pair(j, carry):
        for h in range(2):
            first_row(2 * j + h)
        return carry

    lax.fori_loop(0, (tt + 2) // 2, first_pair, 0)
    for side, outer, inner, into, ok in (
        (pleft, q2.at[0], sp.at[0], fleft, lon > 0),
        (pright, q2.at[1], sp.at[3], fright, lon < n_lon - 1),
    ):
        near = [side[:, 7 : 7 + tt, :], side[:, 9 : 9 + tt, :], outer[...], inner[...]]
        c = side[:, 8 : 8 + tt, :]
        out = apply_step(c[:fields], [x[:fields] for x in near], c[fields], [x[fields] for x in near], mb)
        keep = jnp.where(ok, 1.0, 0.0)
        into[...] = out * keep

    other = lax.rem(me + 1, n_dev)
    all_dest = send_to(other, ds.at[0 : n_dev - 1], rd.at[0 : n_dev - 1], dest_send, dest_recv)
    all_vals = send_to(other, vs.at[0 : n_dev - 1], rv.at[0 : n_dev - 1], val_send, val_recv)
    all_dest.wait_recv()
    all_vals.wait_recv()

    face_p, face_t = helio.shape[1], helio.shape[2]
    acc[...] = jnp.zeros(acc.shape, F32)

    def land(i, carry):
        cell = jnp.concatenate([rd[i * LAND + k] for k in range(LAND)], axis=1).astype(jnp.int32) - 1
        val = jnp.concatenate([rv[i * LAND + k] for k in range(LAND)], axis=1)
        hi = val.astype(BF16).astype(F32)
        on_p = iota((face_p, LAND * LANES), 0) == (cell >> 7)
        on_t = jnp.where(iota((face_t, LAND * LANES), 0) == (cell & 127), 1.0, 0.0).astype(BF16)
        spread = jnp.concatenate(
            [jnp.where(on_p, x[f : f + 1], 0.0).astype(BF16) for x in (hi, val - hi) for f in range(fields)],
            axis=0,
        )
        acc[...] += dot_t(spread, on_t)
        return carry

    lax.fori_loop(0, n_dev // LAND, land, 0)
    half = fields * face_p
    flat = helio[...].reshape(half, face_t) + (acc[0:half] + acc[half:])
    coupled = flat.reshape(fields, face_p, face_t)

    for f in range(fields):
        hs[0, f : f + 1, :] = coupled[f, 0:1, :]
        hs[1, f : f + 1, :] = coupled[f, face_p - 1 : face_p, :]
    row8, lane8 = iota((8, face_t), 0), iota((8, face_t), 1)
    pick = jnp.where(
        ((row8 == 0) & (lane8 == 0)) | ((row8 == 1) & (lane8 == face_t - 1)), 1.0, 0.0
    )
    ts[...] = lax.dot_general(
        pick, flat, (((1,), (1,)), ((), ())), precision=lax.Precision.HIGHEST, preferred_element_type=F32
    )
    edges = [
        ((0, 1), hs.at[1], hr.at[0]),
        ((0, -1), hs.at[0], hr.at[1]),
        ((1, 0), ts, tr.at[0]),
        ((-1, 0), ts, tr.at[1]),
    ]
    launch(edges, face_send, face_recv)

    def second_row(t):
        c = first[:, t + 1]
        low, high = shift_rows(c, fleft[:, pl.ds(t, 1), :], fright[:, pl.ds(t, 1), :])
        kc = ue[fields:, t + 2]
        klow, khigh = shift_rows(
            kc, pleft[fields:, pl.ds(8 + t, 1), :], pright[fields:, pl.ds(8 + t, 1), :]
        )
        out = apply_step(
            c, [first[:, t], first[:, t + 2], low, high],
            kc[0], [ue[fields, t + 1], ue[fields, t + 3], klow[0], khigh[0]], mb,
        )
        st[:, t] = out

    def second_pair(j, carry):
        for h in range(2):
            second_row(2 * j + h)
        return carry

    writes = []
    for h in range(2):
        part = slice(h * (tt // 2), (h + 1) * (tt // 2))
        lax.fori_loop(part.start // 2, part.stop // 2, second_pair, 0)
        writes.append(pltpu.make_async_copy(st.at[:, part], stepped.at[:, part], out_sem.at[h]))
        writes[h].start()

    lane3 = iota(coupled.shape, 2)
    inner = (
        jnp.where(lane3 == 0, 0.0, pltpu.roll(coupled, 1, 2))
        + jnp.where(lane3 == face_t - 1, 0.0, pltpu.roll(coupled, face_t - 1, 2))
        - 4.0 * coupled
    )
    arrive(edges, face_send, face_recv)
    lows = jnp.concatenate([hr[0, f : f + 1, :][None] for f in range(fields)], axis=0)
    highs = jnp.concatenate([hr[1, f : f + 1, :][None] for f in range(fields)], axis=0)
    down, up = shift_rows(coupled, lows, highs)
    put_low = jnp.where((row8 == 1) & (lane8 == 0), 1.0, 0.0)
    put_high = jnp.where((row8 == 0) & (lane8 == face_t - 1), 1.0, 0.0)
    both = jnp.concatenate([tr[0], tr[1]], axis=0)
    sides = lax.dot_general(
        both, jnp.concatenate([put_low, put_high], axis=0), (((0,), (0,)), ((), ())),
        precision=lax.Precision.HIGHEST, preferred_element_type=F32,
    ).reshape(coupled.shape)
    face[...] = coupled + 0.2 * (inner + (down + up) + sides)
    write_face = pltpu.make_async_copy(face, face_out, face_sem)
    write_face.start()

    leave(small, small_send, small_recv)
    leave(moves, halo_send, halo_recv)
    leave(edges, face_send, face_recv)
    all_dest.wait_send()
    all_vals.wait_send()
    for copy in writes:
        copy.wait()
    write_face.wait()


def body(corona, kappa, mixing, helio_prev, owner, dest_cell, corner_base, fractions):
    n_lat, n_lon = lax.axis_size("lat"), lax.axis_size("lon")
    n_dev = n_lat * n_lon
    fields, tt, pp, n_r = corona.shape
    count = corner_base.shape[0]
    face_p, face_t = helio_prev.shape[1:]
    ext = fields + 1
    hbm = pl.BlockSpec(memory_space=pltpu.HBM)
    free = pl.BlockSpec(memory_space=pl.ANY)
    sem = pltpu.SemaphoreType.DMA
    v = lambda *shape: pltpu.VMEM(shape, F32)
    return pl.pallas_call(
        functools.partial(kernel, n_lat, n_lon),
        out_shape=(
            jax.ShapeDtypeStruct(corona.shape, F32),
            jax.ShapeDtypeStruct(helio_prev.shape, F32),
        ),
        in_specs=[hbm] * 8,
        out_specs=(free, free),
        scratch_shapes=[
            pltpu.SMEM(mixing.shape, F32),
            v(*mixing.shape),
            v(fields, fields, 8, LANES),
            v(*helio_prev.shape),
            pltpu.VMEM((1, count), jnp.int32),
            pltpu.VMEM((1, count), jnp.int32),
            pltpu.VMEM((1, count), jnp.int32),
            v(3, count),
            v(*helio_prev.shape),
            v(tt + 4, fields, WIDE),
            v(tt + 4, 1, WIDE),
            v(tt + 2, fields, WIDE),
            v(tt + 2, fields, WIDE),
            v(7, tt + 2, 1, WIDE),
            v(ext, tt + 4, pp, n_r),
            v(4, ext, tt, n_r),
            v(ext, tt + 16, n_r),
            v(ext, tt + 16, n_r),
            v(2, ext, tt, n_r),
            v(4, 16, n_r),
            v(4, 16, n_r),
            v(fields, tt + 2, pp, n_r),
            v(fields, tt, n_r),
            v(fields, tt, n_r),
            v(fields, tt, pp, n_r),
            v(n_dev // GROUP, NPAR, GROUP, LANES),
            v(n_dev, 1, LANES),
            v(n_dev, 1, LANES),
            v(n_dev, fields, LANES),
            v(n_dev, fields, LANES),
            v(tt, fields, 2 * LANES),
            v(2, fields, face_t),
            v(2, fields, face_t),
            v(8, fields * face_p),
            v(2, 8, fields * face_p),
            v(2 * fields * face_p, face_t),
            sem((9,)), sem((10,)), sem((10,)), sem((16,)), sem((16,)), sem((2,)), sem,
            sem, sem, sem, sem, sem((4,)), sem((4,)),
        ],
        compiler_params=pltpu.CompilerParams(
            collective_id=0, has_side_effects=True, vmem_limit_bytes=48 * 1024 * 1024
        ),
        name="corona_helio",
    )(
        *[
            pltpu.with_memory_space_constraint(x, pltpu.HBM)
            for x in (
                corona, kappa, mixing, helio_prev, owner.reshape(1, count), dest_cell.reshape(1, count),
                corner_base.reshape(1, count), fractions,
            )
        ]
    )


def solution(mesh):
    return jax.shard_map(
        body,
        mesh=mesh,
        in_specs=(
            P(None, "lat", "lon", None),
            P("lat", "lon", None),
            P(),
            P(None, "lon", "lat"),
            P(("lat", "lon"), None),
            P(("lat", "lon")),
            P(("lat", "lon")),
            P(None, ("lat", "lon")),
        ),
        out_specs=(P(None, "lat", "lon", None), P(None, "lon", "lat")),
        check_vma=False,
    )
```

```python
import functools

import jax
import jax.numpy as jnp
from jax import lax
from jax.experimental import pallas as pl
from jax.experimental.pallas import tpu as pltpu
from jax.sharding import PartitionSpec as P

SH = 8
F32 = jnp.float32
BF16 = jnp.bfloat16
MESH = pl.DeviceIdType.MESH
LANES = 128
GROUP = 8
LAND = 8
NPAR = 5
DEEP = 16
WIDE = 4 * LANES


def iota(shape, dim):
    return lax.broadcasted_iota(jnp.int32, shape, dim)


def split(x):
    hi = x.astype(BF16)
    return hi, (x - hi.astype(F32)).astype(BF16)


def dot_t(a, b):
    return lax.dot_general(a, b, (((1,), (1,)), ((), ())), preferred_element_type=F32)


def apply_step(c, near, kc, knear, mb):
    lane = iota(kc.shape, 1)
    last = kc.shape[1] - 1
    ks = [0.075 * (kc + kn) for kn in knear]
    kl = 0.075 * (kc + jnp.where(lane == 0, 0.0, pltpu.roll(kc, 1, 1)))
    kr = 0.075 * (kc + jnp.where(lane == last, 0.0, pltpu.roll(kc, last, 1)))
    diag = 1.0 - (((ks[0] + ks[1]) + (ks[2] + ks[3])) + (kl + kr))
    kl = jnp.where(lane == 0, 0.0, kl)
    kr = jnp.where(lane == last, 0.0, kr)
    total = diag[None] * c
    for k, u in zip(ks, near):
        total = total + k[None] * u
    total = total + kl[None] * pltpu.roll(c, 1, 2) + kr[None] * pltpu.roll(c, last, 2)
    tiles = (c.shape[1] // 8, 8, c.shape[2])
    total = total.reshape((c.shape[0],) + tiles)
    for f in range(c.shape[0]):
        total = total + mb[f][:, None] * c[f].reshape(tiles)[None]
    return total.reshape(c.shape)


def shift_rows(c, low, high):
    n = c.shape[1]
    row = iota(c.shape, 1)
    down = jnp.where(row == 0, low, pltpu.roll(c, 1, 1))
    up = jnp.where(row == n - 1, high, pltpu.roll(c, n - 1, 1))
    return down, up


def kernel(
    n_lat, n_lon, corona, kappa, mix_in, helio_in, owner_in, dest_in, base_in, frac_in, stepped, face_out,
    mix, mixv, mb, helio, owner, dest, base, frac, face, xe, ke, xm, xf, co, ue, sp, pleft, pright, q2, cs, cr, first, fleft, fright, st, pk, ds, rd, vs, rv,
    shell, hs, hr, ts, tr, acc, load_sem, halo_send, halo_recv, small_send, small_recv, out_sem, face_sem,
    dest_send, dest_recv, val_send, val_recv, face_send, face_recv,
):
    n_dev = n_lat * n_lon
    fields = corona.shape[0]
    tt, pp = corona.shape[1], corona.shape[2]
    count = owner.shape[1]
    lat, lon = lax.axis_index("lat"), lax.axis_index("lon")
    me = lat * n_lon + lon

    loads = [
        pltpu.make_async_copy(corona, ue.at[0:fields, 2 : 2 + tt], load_sem.at[0]),
        pltpu.make_async_copy(kappa, ue.at[fields, 2 : 2 + tt], load_sem.at[1]),
    ] + [
        pltpu.make_async_copy(src, dst, load_sem.at[2 + k])
        for k, (src, dst) in enumerate(
            ((owner_in, owner), (base_in, base), (frac_in, frac), (dest_in, dest), (mix_in, mix), (mix_in, mixv), (helio_in, helio))
        )
    ]
    for copy in loads:
        copy.start()

    barrier = pltpu.get_barrier_semaphore()

    def greet(i, carry):
        o = lax.rem(me + i, n_dev)
        pl.semaphore_signal(
            barrier, inc=1, device_id=(lax.div(o, n_lon), lax.rem(o, n_lon)), device_id_type=MESH
        )
        return carry

    lax.fori_loop(1, n_dev, greet, 0)
    for copy in loads[:2]:
        copy.wait()

    per = LANES // DEEP
    lane1 = iota((1, LANES), 1)

    def extract(i, carry):
        lane = iota((fields, LANES), 1) // DEEP
        for t in [4 * i + k for k in range(4)]:
            for h in range(pp // per):
                row = jnp.zeros((fields, LANES), F32)
                for j in range(per):
                    x = pltpu.roll(ue[0:fields, t + 2, h * per + j, :], (j + 1) * DEEP % LANES, 1)
                    row = jnp.where(lane == j, x, row)
                xe[t + 2, :, (h + 1) * LANES : (h + 2) * LANES] = row
        return carry

    lax.fori_loop(0, tt // 4, extract, 0)
    lane_t = iota((tt, LANES), 1) // DEEP
    for h in range(pp // per):
        row = jnp.zeros((tt, LANES), F32)
        for j in range(per):
            x = pltpu.roll(ue[fields, 2 : 2 + tt, h * per + j, :], (j + 1) * DEEP % LANES, 1)
            row = jnp.where(lane_t == j, x, row)
        ke[2 : 2 + tt, :, (h + 1) * LANES : (h + 2) * LANES] = row[:, None, :]
    for ref in (xe, ke):
        for t in (0, tt + 3):
            for lo in (0, WIDE - LANES):
                ref[t, :, lo : lo + LANES] = jnp.zeros((ref.shape[1], LANES), F32)

    corners = [(1, 1), (1, -1), (-1, 1), (-1, -1)]
    moves = [
        ((1, 0), ue.at[:, tt : tt + 2], ue.at[:, 0:2]),
        ((-1, 0), ue.at[:, 2:4], ue.at[:, tt + 2 : tt + 4]),
        ((0, 1), sp.at[3], pleft.at[:, 8 : 8 + tt]),
        ((0, 1), sp.at[2], q2.at[0]),
        ((0, -1), sp.at[0], pright.at[:, 8 : 8 + tt]),
        ((0, -1), sp.at[1], q2.at[1]),
    ] + [(ab, cs.at[k], cr.at[k]) for k, ab in enumerate(corners)]

    mid = slice(LANES, WIDE - LANES)
    rows_in = slice(2, 2 + tt)
    places = [
        ((1, 0), (slice(tt, tt + 2), mid), (slice(0, 2), mid)),
        ((-1, 0), (slice(2, 4), mid), (slice(tt + 2, tt + 4), mid)),
        ((0, 1), (rows_in, slice(2 * LANES, 3 * LANES)), (rows_in, slice(0, LANES))),
        ((0, -1), (rows_in, slice(LANES, 2 * LANES)), (rows_in, slice(3 * LANES, WIDE))),
    ]
    for a, b in corners:
        src_t = slice(tt + 1, tt + 2) if a > 0 else slice(2, 3)
        dst_t = slice(1, 2) if a > 0 else slice(tt + 2, tt + 3)
        src_l = slice(2 * LANES, 3 * LANES) if b > 0 else slice(LANES, 2 * LANES)
        dst_l = slice(0, LANES) if b > 0 else slice(3 * LANES, WIDE)
        places.append(((a, b), (src_t, src_l), (dst_t, dst_l)))
    small = [
        (ab, ref.at[src[0], :, src[1]], ref.at[dst[0], :, dst[1]])
        for ab, src, dst in places
        for ref in (xe, ke)
    ]

    def inside(a, b):
        ok = lat >= 0
        if a > 0:
            ok = ok & (lat < n_lat - 1)
        if a < 0:
            ok = ok & (lat > 0)
        if b > 0:
            ok = ok & (lon < n_lon - 1)
        if b < 0:
            ok = ok & (lon > 0)
        return ok

    def remote(a, b, src, dst, send, recv):
        return pltpu.make_async_remote_copy(
            src_ref=src, dst_ref=dst, send_sem=send, recv_sem=recv,
            device_id=(lat + a, lon + b), device_id_type=MESH,
        )

    def launch(todo, send, recv):
        for k, ((a, b), src, dst) in enumerate(todo):

            @pl.when(inside(a, b))
            def _(k=k, a=a, b=b, src=src, dst=dst):
                remote(a, b, src, dst, send.at[k], recv.at[k]).start()

            @pl.when(jnp.logical_not(inside(-a, -b)))
            def _(dst=dst):
                dst[...] = jnp.zeros(dst.shape, F32)

    def arrive(todo, send, recv):
        for k, ((a, b), src, dst) in enumerate(todo):

            @pl.when(inside(-a, -b))
            def _(k=k, a=a, b=b, src=src, dst=dst):
                remote(-a, -b, src, dst, send.at[k], recv.at[k]).wait_recv()

    def leave(todo, send, recv):
        for k, ((a, b), src, dst) in enumerate(todo):

            @pl.when(inside(a, b))
            def _(k=k, a=a, b=b, src=src, dst=dst):
                remote(a, b, src, dst, send.at[k], recv.at[k]).wait_send()

    pl.semaphore_wait(barrier, n_dev - 1)
    launch(small, small_send, small_recv)
    for j, p in enumerate((0, 1, pp - 2, pp - 1)):
        sp[j] = ue[:, 2 : 2 + tt, p, :]
    for k, (a, b) in enumerate(corners):
        t, p = (2 + tt - 1 if a > 0 else 2), (pp - 1 if b > 0 else 0)
        for f in range(fields + 1):
            cs[k, f : f + 1, :] = ue[f, t, p : p + 1, :]

    launch(moves, halo_send, halo_recv)

    for copy in loads[2:]:
        copy.wait()

    for f in range(fields):
        for g in range(fields):
            mb[f, g] = jnp.full((8, LANES), 0.3 * mix[g, f], F32)

    own = owner[...]
    upper = (iota((LANES, LANES), 0) < iota((LANES, LANES), 1)).astype(F32).astype(BF16)
    carry = jnp.zeros((n_dev, 1), F32)
    ranks = []
    for blk in range(count // LANES):
        hit = jnp.where(
            iota((n_dev, LANES), 0) == own[:, blk * LANES : (blk + 1) * LANES], 1.0, 0.0
        )
        before = jnp.dot(hit.astype(BF16), upper, preferred_element_type=F32) + carry
        ranks.append(jnp.sum(hit * before, axis=0, keepdims=True))
        carry = carry + jnp.sum(hit, axis=1, keepdims=True)
    rank = jnp.concatenate(ranks, axis=1).astype(jnp.int32)
    rank_hot = jnp.where(iota((LANES, count), 0) == rank, 1.0, 0.0).astype(BF16)
    rows = [base[...].astype(F32)] + [frac[i : i + 1, :] for i in range(3)]
    rows.append((dest[...] + 1).astype(F32))
    pieces = []
    for row in rows:
        hi = row.astype(BF16).astype(F32)
        pieces += [hi, row - hi]
    chunk = 32

    def place(g, carry):
        mask = iota((chunk, count), 0) + g * chunk == own
        left = jnp.concatenate([jnp.where(mask, x, 0.0).astype(BF16) for x in pieces], axis=0)
        got = dot_t(left, rank_hot)
        for q in range(NPAR):
            val = got[2 * q * chunk : (2 * q + 1) * chunk] + got[(2 * q + 1) * chunk : (2 * q + 2) * chunk]
            for oc in range(chunk // GROUP):
                pk[g * (chunk // GROUP) + oc, q] = val[oc * GROUP : (oc + 1) * GROUP]
            if q == NPAR - 1:
                for o in range(chunk):
                    ds[g * chunk + o] = val[o : o + 1]
        return carry

    lax.fori_loop(0, n_dev // chunk, place, 0)

    def send_to(o, src, dst, send, recv):
        return pltpu.make_async_remote_copy(
            src_ref=src, dst_ref=dst, send_sem=send, recv_sem=recv,
            device_id=(lax.div(o, n_lon), lax.rem(o, n_lon)), device_id_type=MESH,
        )

    def send_dest(i, carry):
        o = lax.rem(me + i, n_dev)
        send_to(o, ds.at[o], rd.at[me], dest_send, dest_recv).start()
        return carry

    lax.fori_loop(1, n_dev, send_dest, 0)
    rd[me] = ds[me]

    nrow = (tt + 2) * fields
    hot = jnp.where(iota((nrow, fields), 0) % fields == iota((nrow, fields), 1), 1.0, 0.0)
    wide_mix = lax.dot_general(
        jnp.dot(hot, 0.3 * mixv[...], precision=lax.Precision.HIGHEST, preferred_element_type=F32),
        hot, (((1,), (1,)), ((), ())), precision=lax.Precision.HIGHEST, preferred_element_type=F32,
    )
    same = iota((nrow, nrow), 0) // fields == iota((nrow, nrow), 1) // fields
    m_hi, m_lo = split(jnp.where(same, wide_mix, 0.0))

    def mixed(x, n):
        hi, lo = split(x)
        mh, ml = m_hi[:n, :n], m_lo[:n, :n]
        dot = lambda a, b: jnp.dot(a, b, preferred_element_type=F32)
        return dot(mh, hi) + (dot(mh, lo) + dot(ml, hi))

    arrive(small, small_send, small_recv)
    xm[...] = mixed(xe[1 : tt + 3].reshape(nrow, WIDE), nrow).reshape(tt + 2, fields, WIDE)
    lane = iota((1, 1, WIDE), 2)
    top = lane % DEEP == DEEP - 1
    outside = ((lane < LANES) & (lon == 0)) | ((lane >= WIDE - LANES) & (lon == n_lon - 1))
    keep_lane = jnp.where(outside, 0.0, 1.0)

    def roll(x, by):
        return pltpu.roll(x, by % WIDE, 2)

    def compact_rows(c, up, down, k):
        return (
            k[6] * c + (k[0] * up + k[1] * down) + (k[2] * roll(c, DEEP) + k[3] * roll(c, -DEEP))
            + (k[4] * roll(c, 1) + k[5] * roll(c, -1))
        )

    def compact_first(j, carry):
        n = 6
        i = j * n
        at = lambda ref, d: ref[pl.ds(i + d, n)]
        kc = at(ke, 1)
        k = [0.075 * (kc + x) for x in (at(ke, 0), at(ke, 2), roll(kc, DEEP), roll(kc, -DEEP), roll(kc, 1))]
        outer = 0.075 * (kc + jnp.where(top, 0.0, roll(kc, -1)))
        diag = 1.0 - (((k[0] + k[1]) + (k[2] + k[3])) + (k[4] + outer))
        k += [jnp.where(top, 0.0, outer), diag]
        row = iota((n, 1, WIDE), 0) + i
        off = ((row == 0) & (lat == 0)) | ((row == tt + 1) & (lat == n_lat - 1))
        keep = jnp.where(off, 0.0, keep_lane)
        xf[pl.ds(i, n)] = keep * (compact_rows(at(xe, 1), at(xe, 0), at(xe, 2), k) + at(xm, 0))
        for q in range(7):
            co[q, pl.ds(i, n)] = k[q]
        return carry

    lax.fori_loop(0, (tt + 2) // 6, compact_first, 0)
    half_wide = 2 * LANES
    again = mixed(xf[1 : tt + 1, :, mid].reshape(tt * fields, half_wide), tt * fields)
    xm[0:tt, :, 0:half_wide] = again.reshape(tt, fields, half_wide)

    def compact_second(j, carry):
        n = 4
        t = j * n
        at = lambda ref, d: ref[pl.ds(t + d, n)]
        k = [co[q, pl.ds(t + 1, n)] for q in range(7)]
        out = compact_rows(at(xf, 1), at(xf, 0), at(xf, 2), k)
        shell[pl.ds(t, n)] = out[:, :, mid] + xm[pl.ds(t, n), :, 0:half_wide]
        return carry

    lax.fori_loop(0, tt // 4, compact_second, 0)
    deep_at, cell_at = iota((2 * LANES, LANES), 0), iota((2 * LANES, LANES), 1)
    take = jnp.where(
        (deep_at // DEEP == cell_at // SH) & (deep_at % DEEP == cell_at % SH + DEEP - SH), 1.0, 0.0
    ).astype(BF16)
    s_hi, s_lo = [
        jnp.dot(x, take, preferred_element_type=F32).astype(BF16)
        for x in split(shell[...].reshape(tt * fields, 2 * LANES))
    ]
    left = jnp.concatenate([s_hi, s_hi, s_lo], axis=1)
    groups = n_dev // GROUP
    wide = GROUP * LANES

    def values(i, carry):
        g = lax.rem(lax.div(me, GROUP) + i, groups)
        par = [
            jnp.concatenate([pk[g, q, k : k + 1, :] for k in range(GROUP)], axis=1)
            for q in range(NPAR - 1)
        ]
        cell = par[0].astype(jnp.int32)
        t0, p0, r0 = cell >> 7, (cell >> 3) & 15, cell & 7
        fx, fy, fz = par[1:]

        def weights(n, at, fr):
            idx = iota((n, wide), 0) - at
            return jnp.where(idx == 0, 1.0 - fr, jnp.where(idx == 1, fr, 0.0))

        wa, wb, wc = weights(tt, t0, fx), weights(pp, p0, fy), weights(SH, r0, fz)
        table = (wb[:, None, :] * wc[None]).reshape(pp * SH, wide)
        hi, lo = split(table)
        got = jnp.dot(left, jnp.concatenate([hi, lo, hi], axis=0), preferred_element_type=F32)
        val = jnp.sum(got.reshape(tt, fields, wide) * wa[:, None, :], axis=0)
        for k in range(GROUP):
            vs[g * GROUP + k] = val[:, k * LANES : (k + 1) * LANES]
        for k in range(GROUP):
            o = g * GROUP + k

            @pl.when(o != me)
            def _(o=o):
                send_to(o, vs.at[o], rv.at[me], val_send, val_recv).start()

        return carry

    lax.fori_loop(0, groups, values, 0)
    rv[me] = vs[me]

    arrive(moves, halo_send, halo_recv)
    for k, (a, b) in enumerate(corners):
        side = pleft if b > 0 else pright
        row = 7 if a > 0 else 8 + tt
        for f in range(fields + 1):
            side[f, row : row + 1, :] = cr[k, f : f + 1, :]

    def first_row(i):
        c = ue[:, i + 1]
        low, high = shift_rows(c, pleft[:, pl.ds(7 + i, 1), :], pright[:, pl.ds(7 + i, 1), :])
        up, down = ue[:, i], ue[:, i + 2]
        out = apply_step(
            c[:fields], [x[:fields] for x in (up, down, low, high)],
            c[fields], [x[fields] for x in (up, down, low, high)], mb,
        )
        first[:, i] = out

    def first_rows(j, carry):
        for h in range(3):
            first_row(3 * j + h)
        return carry

    lax.fori_loop(0, (tt + 2) // 3, first_rows, 0)
    for i, edge in ((0, 0), (tt + 1, n_lat - 1)):

        @pl.when(lat == edge)
        def _(i=i):
            first[:, i] = jnp.zeros((fields, pp, first.shape[3]), F32)

    for side, outer, inner, into, ok in (
        (pleft, q2.at[0], sp.at[0], fleft, lon > 0),
        (pright, q2.at[1], sp.at[3], fright, lon < n_lon - 1),
    ):
        near = [side[:, 7 : 7 + tt, :], side[:, 9 : 9 + tt, :], outer[...], inner[...]]
        c = side[:, 8 : 8 + tt, :]
        out = apply_step(c[:fields], [x[:fields] for x in near], c[fields], [x[fields] for x in near], mb)
        keep = jnp.where(ok, 1.0, 0.0)
        into[...] = out * keep

    other = lax.rem(me + 1, n_dev)
    all_dest = send_to(other, ds.at[0 : n_dev - 1], rd.at[0 : n_dev - 1], dest_send, dest_recv)
    all_vals = send_to(other, vs.at[0 : n_dev - 1], rv.at[0 : n_dev - 1], val_send, val_recv)
    all_dest.wait_recv()
    all_vals.wait_recv()

    face_p, face_t = helio.shape[1], helio.shape[2]
    acc[...] = jnp.zeros(acc.shape, F32)

    def land(i, carry):
        cell = jnp.concatenate([rd[i * LAND + k] for k in range(LAND)], axis=1).astype(jnp.int32) - 1
        val = jnp.concatenate([rv[i * LAND + k] for k in range(LAND)], axis=1)
        hi = val.astype(BF16).astype(F32)
        on_p = iota((face_p, LAND * LANES), 0) == (cell >> 7)
        on_t = jnp.where(iota((face_t, LAND * LANES), 0) == (cell & 127), 1.0, 0.0).astype(BF16)
        spread = jnp.concatenate(
            [jnp.where(on_p, x[f : f + 1], 0.0).astype(BF16) for x in (hi, val - hi) for f in range(fields)],
            axis=0,
        )
        acc[...] += dot_t(spread, on_t)
        return carry

    lax.fori_loop(0, n_dev // LAND, land, 0)
    half = fields * face_p
    flat = helio[...].reshape(half, face_t) + (acc[0:half] + acc[half:])
    coupled = flat.reshape(fields, face_p, face_t)

    for f in range(fields):
        hs[0, f : f + 1, :] = coupled[f, 0:1, :]
        hs[1, f : f + 1, :] = coupled[f, face_p - 1 : face_p, :]
    row8, lane8 = iota((8, face_t), 0), iota((8, face_t), 1)
    pick = jnp.where(
        ((row8 == 0) & (lane8 == 0)) | ((row8 == 1) & (lane8 == face_t - 1)), 1.0, 0.0
    )
    ts[...] = lax.dot_general(
        pick, flat, (((1,), (1,)), ((), ())), precision=lax.Precision.HIGHEST, preferred_element_type=F32
    )
    edges = [
        ((0, 1), hs.at[1], hr.at[0]),
        ((0, -1), hs.at[0], hr.at[1]),
        ((1, 0), ts, tr.at[0]),
        ((-1, 0), ts, tr.at[1]),
    ]
    launch(edges, face_send, face_recv)

    def second_row(t):
        c = first[:, t + 1]
        low, high = shift_rows(c, fleft[:, pl.ds(t, 1), :], fright[:, pl.ds(t, 1), :])
        kc = ue[fields:, t + 2]
        klow, khigh = shift_rows(
            kc, pleft[fields:, pl.ds(8 + t, 1), :], pright[fields:, pl.ds(8 + t, 1), :]
        )
        out = apply_step(
            c, [first[:, t], first[:, t + 2], low, high],
            kc[0], [ue[fields, t + 1], ue[fields, t + 3], klow[0], khigh[0]], mb,
        )
        st[:, t] = out

    def second_rows(j, carry):
        for h in range(4):
            second_row(4 * j + h)
        return carry

    writes = []
    for h in range(2):
        part = slice(h * (tt // 2), (h + 1) * (tt // 2))
        lax.fori_loop(part.start // 4, part.stop // 4, second_rows, 0)
        writes.append(pltpu.make_async_copy(st.at[:, part], stepped.at[:, part], out_sem.at[h]))
        writes[h].start()

    lane3 = iota(coupled.shape, 2)
    inner = (
        jnp.where(lane3 == 0, 0.0, pltpu.roll(coupled, 1, 2))
        + jnp.where(lane3 == face_t - 1, 0.0, pltpu.roll(coupled, face_t - 1, 2))
        - 4.0 * coupled
    )
    arrive(edges, face_send, face_recv)
    lows = jnp.concatenate([hr[0, f : f + 1, :][None] for f in range(fields)], axis=0)
    highs = jnp.concatenate([hr[1, f : f + 1, :][None] for f in range(fields)], axis=0)
    down, up = shift_rows(coupled, lows, highs)
    put_low = jnp.where((row8 == 1) & (lane8 == 0), 1.0, 0.0)
    put_high = jnp.where((row8 == 0) & (lane8 == face_t - 1), 1.0, 0.0)
    both = jnp.concatenate([tr[0], tr[1]], axis=0)
    sides = lax.dot_general(
        both, jnp.concatenate([put_low, put_high], axis=0), (((0,), (0,)), ((), ())),
        precision=lax.Precision.HIGHEST, preferred_element_type=F32,
    ).reshape(coupled.shape)
    face[...] = coupled + 0.2 * (inner + (down + up) + sides)
    write_face = pltpu.make_async_copy(face, face_out, face_sem)
    write_face.start()

    leave(small, small_send, small_recv)
    leave(moves, halo_send, halo_recv)
    leave(edges, face_send, face_recv)
    all_dest.wait_send()
    all_vals.wait_send()
    for copy in writes:
        copy.wait()
    write_face.wait()


def body(corona, kappa, mixing, helio_prev, owner, dest_cell, corner_base, fractions):
    n_lat, n_lon = lax.axis_size("lat"), lax.axis_size("lon")
    n_dev = n_lat * n_lon
    fields, tt, pp, n_r = corona.shape
    count = corner_base.shape[0]
    face_p, face_t = helio_prev.shape[1:]
    ext = fields + 1
    hbm = pl.BlockSpec(memory_space=pltpu.HBM)
    free = pl.BlockSpec(memory_space=pl.ANY)
    sem = pltpu.SemaphoreType.DMA
    v = lambda *shape: pltpu.VMEM(shape, F32)
    return pl.pallas_call(
        functools.partial(kernel, n_lat, n_lon),
        out_shape=(
            jax.ShapeDtypeStruct(corona.shape, F32),
            jax.ShapeDtypeStruct(helio_prev.shape, F32),
        ),
        in_specs=[hbm] * 8,
        out_specs=(free, free),
        scratch_shapes=[
            pltpu.SMEM(mixing.shape, F32),
            v(*mixing.shape),
            v(fields, fields, 8, LANES),
            v(*helio_prev.shape),
            pltpu.VMEM((1, count), jnp.int32),
            pltpu.VMEM((1, count), jnp.int32),
            pltpu.VMEM((1, count), jnp.int32),
            v(3, count),
            v(*helio_prev.shape),
            v(tt + 4, fields, WIDE),
            v(tt + 4, 1, WIDE),
            v(tt + 2, fields, WIDE),
            v(tt + 2, fields, WIDE),
            v(7, tt + 2, 1, WIDE),
            v(ext, tt + 4, pp, n_r),
            v(4, ext, tt, n_r),
            v(ext, tt + 16, n_r),
            v(ext, tt + 16, n_r),
            v(2, ext, tt, n_r),
            v(4, 16, n_r),
            v(4, 16, n_r),
            v(fields, tt + 2, pp, n_r),
            v(fields, tt, n_r),
            v(fields, tt, n_r),
            v(fields, tt, pp, n_r),
            v(n_dev // GROUP, NPAR, GROUP, LANES),
            v(n_dev, 1, LANES),
            v(n_dev, 1, LANES),
            v(n_dev, fields, LANES),
            v(n_dev, fields, LANES),
            v(tt, fields, 2 * LANES),
            v(2, fields, face_t),
            v(2, fields, face_t),
            v(8, fields * face_p),
            v(2, 8, fields * face_p),
            v(2 * fields * face_p, face_t),
            sem((9,)), sem((10,)), sem((10,)), sem((16,)), sem((16,)), sem((2,)), sem,
            sem, sem, sem, sem, sem((4,)), sem((4,)),
        ],
        compiler_params=pltpu.CompilerParams(
            collective_id=0, has_side_effects=True, vmem_limit_bytes=48 * 1024 * 1024
        ),
        name="corona_helio",
    )(
        *[
            pltpu.with_memory_space_constraint(x, pltpu.HBM)
            for x in (
                corona, kappa, mixing, helio_prev, owner.reshape(1, count), dest_cell.reshape(1, count),
                corner_base.reshape(1, count), fractions,
            )
        ]
    )


def solution(mesh):
    return jax.shard_map(
        body,
        mesh=mesh,
        in_specs=(
            P(None, "lat", "lon", None),
            P("lat", "lon", None),
            P(),
            P(None, "lon", "lat"),
            P(("lat", "lon"), None),
            P(("lat", "lon")),
            P(("lat", "lon")),
            P(None, ("lat", "lon")),
        ),
        out_specs=(P(None, "lat", "lon", None), P(None, "lon", "lat")),
        check_vma=False,
    )
```

```python
import functools

import jax
import jax.numpy as jnp
from jax import lax
from jax.experimental import pallas as pl
from jax.experimental.pallas import tpu as pltpu
from jax.sharding import PartitionSpec as P

SH = 8
F32 = jnp.float32
BF16 = jnp.bfloat16
MESH = pl.DeviceIdType.MESH
LANES = 128
GROUP = 8
LAND = 8
NPAR = 5
DEEP = 16
WIDE = 4 * LANES


def iota(shape, dim):
    return lax.broadcasted_iota(jnp.int32, shape, dim)


def split(x):
    hi = x.astype(BF16)
    return hi, (x - hi.astype(F32)).astype(BF16)


def dot_t(a, b):
    return lax.dot_general(a, b, (((1,), (1,)), ((), ())), preferred_element_type=F32)


def apply_step(c, near, kc, knear, mb):
    lane = iota(kc.shape, 1)
    last = kc.shape[1] - 1
    ks = [0.075 * (kc + kn) for kn in knear]
    kl = 0.075 * (kc + jnp.where(lane == 0, 0.0, pltpu.roll(kc, 1, 1)))
    kr = 0.075 * (kc + jnp.where(lane == last, 0.0, pltpu.roll(kc, last, 1)))
    diag = 1.0 - (((ks[0] + ks[1]) + (ks[2] + ks[3])) + (kl + kr))
    kl = jnp.where(lane == 0, 0.0, kl)
    kr = jnp.where(lane == last, 0.0, kr)
    total = diag[None] * c
    for k, u in zip(ks, near):
        total = total + k[None] * u
    total = total + kl[None] * pltpu.roll(c, 1, 2) + kr[None] * pltpu.roll(c, last, 2)
    tiles = (c.shape[1] // 8, 8, c.shape[2])
    total = total.reshape((c.shape[0],) + tiles)
    for f in range(c.shape[0]):
        total = total + mb[f][:, None] * c[f].reshape(tiles)[None]
    return total.reshape(c.shape)


def shift_rows(c, low, high):
    n = c.shape[1]
    row = iota(c.shape, 1)
    down = jnp.where(row == 0, low, pltpu.roll(c, 1, 1))
    up = jnp.where(row == n - 1, high, pltpu.roll(c, n - 1, 1))
    return down, up


def kernel(
    n_lat, n_lon, corona, kappa, mix_in, helio_in, owner_in, dest_in, base_in, frac_in, stepped, face_out,
    mix, mixv, mb, helio, owner, dest, base, frac, face, xe, ke, xm, xf, co, ue, sp, pleft, pright, q2, cs, cr, first, fleft, fright, st, pk, ds, rd, vs, rv,
    shell, hs, hr, ts, tr, acc, load_sem, halo_send, halo_recv, small_send, small_recv, out_sem, face_sem,
    dest_send, dest_recv, val_send, val_recv, face_send, face_recv,
):
    n_dev = n_lat * n_lon
    fields = corona.shape[0]
    tt, pp = corona.shape[1], corona.shape[2]
    count = owner.shape[1]
    lat, lon = lax.axis_index("lat"), lax.axis_index("lon")
    me = lat * n_lon + lon

    loads = [
        pltpu.make_async_copy(corona, ue.at[0:fields, 2 : 2 + tt], load_sem.at[0]),
        pltpu.make_async_copy(kappa, ue.at[fields, 2 : 2 + tt], load_sem.at[1]),
    ] + [
        pltpu.make_async_copy(src, dst, load_sem.at[2 + k])
        for k, (src, dst) in enumerate(
            ((owner_in, owner), (base_in, base), (frac_in, frac), (dest_in, dest), (mix_in, mix), (mix_in, mixv), (helio_in, helio))
        )
    ]
    for copy in loads:
        copy.start()

    barrier = pltpu.get_barrier_semaphore()

    def greet(i, carry):
        o = lax.rem(me + i, n_dev)
        pl.semaphore_signal(
            barrier, inc=1, device_id=(lax.div(o, n_lon), lax.rem(o, n_lon)), device_id_type=MESH
        )
        return carry

    lax.fori_loop(1, n_dev, greet, 0)
    for copy in loads[:2]:
        copy.wait()

    per = LANES // DEEP
    lane1 = iota((1, LANES), 1)

    def extract(i, carry):
        lane = iota((fields, LANES), 1) // DEEP
        for t in [4 * i + k for k in range(4)]:
            for h in range(pp // per):
                row = jnp.zeros((fields, LANES), F32)
                for j in range(per):
                    x = pltpu.roll(ue[0:fields, t + 2, h * per + j, :], (j + 1) * DEEP % LANES, 1)
                    row = jnp.where(lane == j, x, row)
                xe[t + 2, :, (h + 1) * LANES : (h + 2) * LANES] = row
        return carry

    lax.fori_loop(0, tt // 4, extract, 0)
    lane_t = iota((tt, LANES), 1) // DEEP
    for h in range(pp // per):
        row = jnp.zeros((tt, LANES), F32)
        for j in range(per):
            x = pltpu.roll(ue[fields, 2 : 2 + tt, h * per + j, :], (j + 1) * DEEP % LANES, 1)
            row = jnp.where(lane_t == j, x, row)
        ke[2 : 2 + tt, :, (h + 1) * LANES : (h + 2) * LANES] = row[:, None, :]
    for ref in (xe, ke):
        for t in (0, tt + 3):
            for lo in (0, WIDE - LANES):
                ref[t, :, lo : lo + LANES] = jnp.zeros((ref.shape[1], LANES), F32)

    corners = [(1, 1), (1, -1), (-1, 1), (-1, -1)]
    moves = [
        ((1, 0), ue.at[:, tt : tt + 2], ue.at[:, 0:2]),
        ((-1, 0), ue.at[:, 2:4], ue.at[:, tt + 2 : tt + 4]),
        ((0, 1), sp.at[3], pleft.at[:, 8 : 8 + tt]),
        ((0, 1), sp.at[2], q2.at[0]),
        ((0, -1), sp.at[0], pright.at[:, 8 : 8 + tt]),
        ((0, -1), sp.at[1], q2.at[1]),
    ] + [(ab, cs.at[k], cr.at[k]) for k, ab in enumerate(corners)]

    mid = slice(LANES, WIDE - LANES)
    rows_in = slice(2, 2 + tt)
    places = [
        ((1, 0), (slice(tt, tt + 2), mid), (slice(0, 2), mid)),
        ((-1, 0), (slice(2, 4), mid), (slice(tt + 2, tt + 4), mid)),
        ((0, 1), (rows_in, slice(2 * LANES, 3 * LANES)), (rows_in, slice(0, LANES))),
        ((0, -1), (rows_in, slice(LANES, 2 * LANES)), (rows_in, slice(3 * LANES, WIDE))),
    ]
    for a, b in corners:
        src_t = slice(tt + 1, tt + 2) if a > 0 else slice(2, 3)
        dst_t = slice(1, 2) if a > 0 else slice(tt + 2, tt + 3)
        src_l = slice(2 * LANES, 3 * LANES) if b > 0 else slice(LANES, 2 * LANES)
        dst_l = slice(0, LANES) if b > 0 else slice(3 * LANES, WIDE)
        places.append(((a, b), (src_t, src_l), (dst_t, dst_l)))
    small = [
        (ab, ref.at[src[0], :, src[1]], ref.at[dst[0], :, dst[1]])
        for ab, src, dst in places
        for ref in (xe, ke)
    ]

    def inside(a, b):
        ok = lat >= 0
        if a > 0:
            ok = ok & (lat < n_lat - 1)
        if a < 0:
            ok = ok & (lat > 0)
        if b > 0:
            ok = ok & (lon < n_lon - 1)
        if b < 0:
            ok = ok & (lon > 0)
        return ok

    def remote(a, b, src, dst, send, recv):
        return pltpu.make_async_remote_copy(
            src_ref=src, dst_ref=dst, send_sem=send, recv_sem=recv,
            device_id=(lat + a, lon + b), device_id_type=MESH,
        )

    def launch(todo, send, recv):
        for k, ((a, b), src, dst) in enumerate(todo):

            @pl.when(inside(a, b))
            def _(k=k, a=a, b=b, src=src, dst=dst):
                remote(a, b, src, dst, send.at[k], recv.at[k]).start()

            @pl.when(jnp.logical_not(inside(-a, -b)))
            def _(dst=dst):
                dst[...] = jnp.zeros(dst.shape, F32)

    def arrive(todo, send, recv):
        for k, ((a, b), src, dst) in enumerate(todo):

            @pl.when(inside(-a, -b))
            def _(k=k, a=a, b=b, src=src, dst=dst):
                remote(-a, -b, src, dst, send.at[k], recv.at[k]).wait_recv()

    def leave(todo, send, recv):
        for k, ((a, b), src, dst) in enumerate(todo):

            @pl.when(inside(a, b))
            def _(k=k, a=a, b=b, src=src, dst=dst):
                remote(a, b, src, dst, send.at[k], recv.at[k]).wait_send()

    pl.semaphore_wait(barrier, n_dev - 1)
    launch(small, small_send, small_recv)
    for j, p in enumerate((0, 1, pp - 2, pp - 1)):
        sp[j] = ue[:, 2 : 2 + tt, p, :]
    for k, (a, b) in enumerate(corners):
        t, p = (2 + tt - 1 if a > 0 else 2), (pp - 1 if b > 0 else 0)
        for f in range(fields + 1):
            cs[k, f : f + 1, :] = ue[f, t, p : p + 1, :]

    launch(moves, halo_send, halo_recv)

    for copy in loads[2:]:
        copy.wait()

    for f in range(fields):
        for g in range(fields):
            mb[f, g] = jnp.full((8, LANES), 0.3 * mix[g, f], F32)

    own = owner[...]
    upper = (iota((LANES, LANES), 0) < iota((LANES, LANES), 1)).astype(F32).astype(BF16)
    carry = jnp.zeros((n_dev, 1), F32)
    ranks = []
    for blk in range(count // LANES):
        hit = jnp.where(
            iota((n_dev, LANES), 0) == own[:, blk * LANES : (blk + 1) * LANES], 1.0, 0.0
        )
        before = jnp.dot(hit.astype(BF16), upper, preferred_element_type=F32) + carry
        ranks.append(jnp.sum(hit * before, axis=0, keepdims=True))
        carry = carry + jnp.sum(hit, axis=1, keepdims=True)
    rank = jnp.concatenate(ranks, axis=1).astype(jnp.int32)
    rank_hot = jnp.where(iota((LANES, count), 0) == rank, 1.0, 0.0).astype(BF16)
    rows = [base[...].astype(F32)] + [frac[i : i + 1, :] for i in range(3)]
    rows.append((dest[...] + 1).astype(F32))
    pieces = []
    for row in rows:
        hi = row.astype(BF16).astype(F32)
        pieces += [hi, row - hi]
    chunk = 32

    def place(g, carry):
        mask = iota((chunk, count), 0) + g * chunk == own
        left = jnp.concatenate([jnp.where(mask, x, 0.0).astype(BF16) for x in pieces], axis=0)
        got = dot_t(left, rank_hot)
        for q in range(NPAR):
            val = got[2 * q * chunk : (2 * q + 1) * chunk] + got[(2 * q + 1) * chunk : (2 * q + 2) * chunk]
            for oc in range(chunk // GROUP):
                pk[g * (chunk // GROUP) + oc, q] = val[oc * GROUP : (oc + 1) * GROUP]
            if q == NPAR - 1:
                for o in range(chunk):
                    ds[g * chunk + o] = val[o : o + 1]
        return carry

    lax.fori_loop(0, n_dev // chunk, place, 0)

    def send_to(o, src, dst, send, recv):
        return pltpu.make_async_remote_copy(
            src_ref=src, dst_ref=dst, send_sem=send, recv_sem=recv,
            device_id=(lax.div(o, n_lon), lax.rem(o, n_lon)), device_id_type=MESH,
        )

    def send_dest(i, carry):
        o = lax.rem(me + i, n_dev)
        send_to(o, ds.at[o], rd.at[me], dest_send, dest_recv).start()
        return carry

    lax.fori_loop(1, n_dev, send_dest, 0)
    rd[me] = ds[me]

    nrow = (tt + 2) * fields
    hot = jnp.where(iota((nrow, fields), 0) % fields == iota((nrow, fields), 1), 1.0, 0.0)
    wide_mix = lax.dot_general(
        jnp.dot(hot, 0.3 * mixv[...], precision=lax.Precision.HIGHEST, preferred_element_type=F32),
        hot, (((1,), (1,)), ((), ())), precision=lax.Precision.HIGHEST, preferred_element_type=F32,
    )
    same = iota((nrow, nrow), 0) // fields == iota((nrow, nrow), 1) // fields
    m_hi, m_lo = split(jnp.where(same, wide_mix, 0.0))

    def mixed(x, n):
        hi, lo = split(x)
        mh, ml = m_hi[:n, :n], m_lo[:n, :n]
        dot = lambda a, b: jnp.dot(a, b, preferred_element_type=F32)
        return dot(mh, hi) + (dot(mh, lo) + dot(ml, hi))

    arrive(small, small_send, small_recv)
    xm[...] = mixed(xe[1 : tt + 3].reshape(nrow, WIDE), nrow).reshape(tt + 2, fields, WIDE)
    lane = iota((1, 1, WIDE), 2)
    top = lane % DEEP == DEEP - 1
    outside = ((lane < LANES) & (lon == 0)) | ((lane >= WIDE - LANES) & (lon == n_lon - 1))
    keep_lane = jnp.where(outside, 0.0, 1.0)

    def roll(x, by):
        return pltpu.roll(x, by % WIDE, 2)

    def compact_rows(c, up, down, k):
        return (
            k[6] * c + (k[0] * up + k[1] * down) + (k[2] * roll(c, DEEP) + k[3] * roll(c, -DEEP))
            + (k[4] * roll(c, 1) + k[5] * roll(c, -1))
        )

    def compact_first(j, carry):
        n = 6
        i = j * n
        at = lambda ref, d: ref[pl.ds(i + d, n)]
        kc = at(ke, 1)
        k = [0.075 * (kc + x) for x in (at(ke, 0), at(ke, 2), roll(kc, DEEP), roll(kc, -DEEP), roll(kc, 1))]
        outer = 0.075 * (kc + jnp.where(top, 0.0, roll(kc, -1)))
        diag = 1.0 - (((k[0] + k[1]) + (k[2] + k[3])) + (k[4] + outer))
        k += [jnp.where(top, 0.0, outer), diag]
        row = iota((n, 1, WIDE), 0) + i
        off = ((row == 0) & (lat == 0)) | ((row == tt + 1) & (lat == n_lat - 1))
        keep = jnp.where(off, 0.0, keep_lane)
        xf[pl.ds(i, n)] = keep * (compact_rows(at(xe, 1), at(xe, 0), at(xe, 2), k) + at(xm, 0))
        for q in range(7):
            co[q, pl.ds(i, n)] = k[q]
        return carry

    lax.fori_loop(0, (tt + 2) // 6, compact_first, 0)
    half_wide = 2 * LANES
    again = mixed(xf[1 : tt + 1, :, mid].reshape(tt * fields, half_wide), tt * fields)
    xm[0:tt, :, 0:half_wide] = again.reshape(tt, fields, half_wide)

    def compact_second(j, carry):
        n = 4
        t = j * n
        at = lambda ref, d: ref[pl.ds(t + d, n)]
        k = [co[q, pl.ds(t + 1, n)] for q in range(7)]
        out = compact_rows(at(xf, 1), at(xf, 0), at(xf, 2), k)
        shell[pl.ds(t, n)] = out[:, :, mid] + xm[pl.ds(t, n), :, 0:half_wide]
        return carry

    lax.fori_loop(0, tt // 4, compact_second, 0)
    deep_at, cell_at = iota((2 * LANES, LANES), 0), iota((2 * LANES, LANES), 1)
    take = jnp.where(
        (deep_at // DEEP == cell_at // SH) & (deep_at % DEEP == cell_at % SH + DEEP - SH), 1.0, 0.0
    ).astype(BF16)
    s_hi, s_lo = [
        jnp.dot(x, take, preferred_element_type=F32).astype(BF16)
        for x in split(shell[...].reshape(tt * fields, 2 * LANES))
    ]
    left = jnp.concatenate(
        [jnp.concatenate([s_hi, s_hi], axis=1), jnp.concatenate([s_lo, jnp.zeros_like(s_lo)], axis=1)], axis=0
    )
    groups = n_dev // GROUP
    wide = GROUP * LANES

    def values(i, carry):
        g = lax.rem(lax.div(me, GROUP) + i, groups)
        par = [
            jnp.concatenate([pk[g, q, k : k + 1, :] for k in range(GROUP)], axis=1)
            for q in range(NPAR - 1)
        ]
        cell = par[0].astype(jnp.int32)
        t0, p0, r0 = cell >> 7, (cell >> 3) & 15, cell & 7
        fx, fy, fz = par[1:]

        def weights(n, at, fr):
            idx = iota((n, wide), 0) - at
            return jnp.where(idx == 0, 1.0 - fr, jnp.where(idx == 1, fr, 0.0))

        wa, wb, wc = weights(tt, t0, fx), weights(pp, p0, fy), weights(SH, r0, fz)
        table = (wb[:, None, :] * wc[None]).reshape(pp * SH, wide)
        hi, lo = split(table)
        got = jnp.dot(left, jnp.concatenate([hi, lo], axis=0), preferred_element_type=F32)
        got = got[: tt * fields] + got[tt * fields :]
        val = jnp.sum(got.reshape(tt, fields, wide) * wa[:, None, :], axis=0)
        for k in range(GROUP):
            vs[g * GROUP + k] = val[:, k * LANES : (k + 1) * LANES]
        for k in range(GROUP):
            o = g * GROUP + k

            @pl.when(o != me)
            def _(o=o):
                send_to(o, vs.at[o], rv.at[me], val_send, val_recv).start()

        return carry

    lax.fori_loop(0, groups, values, 0)
    rv[me] = vs[me]

    arrive(moves, halo_send, halo_recv)
    for k, (a, b) in enumerate(corners):
        side = pleft if b > 0 else pright
        row = 7 if a > 0 else 8 + tt
        for f in range(fields + 1):
            side[f, row : row + 1, :] = cr[k, f : f + 1, :]

    def first_row(i):
        c = ue[:, i + 1]
        low, high = shift_rows(c, pleft[:, pl.ds(7 + i, 1), :], pright[:, pl.ds(7 + i, 1), :])
        up, down = ue[:, i], ue[:, i + 2]
        out = apply_step(
            c[:fields], [x[:fields] for x in (up, down, low, high)],
            c[fields], [x[fields] for x in (up, down, low, high)], mb,
        )
        first[:, i] = out

    def first_rows(j, carry):
        for h in range(3):
            first_row(3 * j + h)
        return carry

    lax.fori_loop(0, (tt + 2) // 3, first_rows, 0)
    for i, edge in ((0, 0), (tt + 1, n_lat - 1)):

        @pl.when(lat == edge)
        def _(i=i):
            first[:, i] = jnp.zeros((fields, pp, first.shape[3]), F32)

    for side, outer, inner, into, ok in (
        (pleft, q2.at[0], sp.at[0], fleft, lon > 0),
        (pright, q2.at[1], sp.at[3], fright, lon < n_lon - 1),
    ):
        near = [side[:, 7 : 7 + tt, :], side[:, 9 : 9 + tt, :], outer[...], inner[...]]
        c = side[:, 8 : 8 + tt, :]
        out = apply_step(c[:fields], [x[:fields] for x in near], c[fields], [x[fields] for x in near], mb)
        keep = jnp.where(ok, 1.0, 0.0)
        into[...] = out * keep

    other = lax.rem(me + 1, n_dev)
    all_dest = send_to(other, ds.at[0 : n_dev - 1], rd.at[0 : n_dev - 1], dest_send, dest_recv)
    all_vals = send_to(other, vs.at[0 : n_dev - 1], rv.at[0 : n_dev - 1], val_send, val_recv)
    all_dest.wait_recv()
    all_vals.wait_recv()

    face_p, face_t = helio.shape[1], helio.shape[2]
    rows_p = face_p // 2
    acc[...] = jnp.zeros(acc.shape, F32)

    def land(i, carry):
        cell = jnp.concatenate([rd[i * LAND + k] for k in range(LAND)], axis=1).astype(jnp.int32) - 1
        val = jnp.concatenate([rv[i * LAND + k] for k in range(LAND)], axis=1)
        hi = val.astype(BF16).astype(F32)
        low_p = jnp.where(cell < 0, -1, (cell >> 7) & (rows_p - 1))
        column = (cell & 127) + (cell >> 11) * face_t
        on_p = iota((rows_p, LAND * LANES), 0) == low_p
        on_t = jnp.where(iota((2 * face_t, LAND * LANES), 0) == column, 1.0, 0.0).astype(BF16)
        spread = jnp.concatenate(
            [jnp.where(on_p, x[f : f + 1], 0.0).astype(BF16) for x in (hi, val - hi) for f in range(fields)],
            axis=0,
        )
        acc[...] += dot_t(spread, on_t)
        return carry

    lax.fori_loop(0, n_dev // LAND, land, 0)
    half = fields * rows_p
    added = (acc[0:half] + acc[half:]).reshape(fields, rows_p, 2 * face_t)
    coupled = helio[...] + jnp.concatenate([added[:, :, :face_t], added[:, :, face_t:]], axis=1)
    flat = coupled.reshape(fields * face_p, face_t)

    for f in range(fields):
        hs[0, f : f + 1, :] = coupled[f, 0:1, :]
        hs[1, f : f + 1, :] = coupled[f, face_p - 1 : face_p, :]
    row8, lane8 = iota((8, face_t), 0), iota((8, face_t), 1)
    pick = jnp.where(
        ((row8 == 0) & (lane8 == 0)) | ((row8 == 1) & (lane8 == face_t - 1)), 1.0, 0.0
    )
    ts[...] = lax.dot_general(
        pick, flat, (((1,), (1,)), ((), ())), precision=lax.Precision.HIGHEST, preferred_element_type=F32
    )
    edges = [
        ((0, 1), hs.at[1], hr.at[0]),
        ((0, -1), hs.at[0], hr.at[1]),
        ((1, 0), ts, tr.at[0]),
        ((-1, 0), ts, tr.at[1]),
    ]
    launch(edges, face_send, face_recv)

    def second_row(t):
        c = first[:, t + 1]
        low, high = shift_rows(c, fleft[:, pl.ds(t, 1), :], fright[:, pl.ds(t, 1), :])
        kc = ue[fields:, t + 2]
        klow, khigh = shift_rows(
            kc, pleft[fields:, pl.ds(8 + t, 1), :], pright[fields:, pl.ds(8 + t, 1), :]
        )
        out = apply_step(
            c, [first[:, t], first[:, t + 2], low, high],
            kc[0], [ue[fields, t + 1], ue[fields, t + 3], klow[0], khigh[0]], mb,
        )
        st[:, t] = out

    def second_rows(j, carry):
        for h in range(4):
            second_row(4 * j + h)
        return carry

    writes = []
    for h in range(2):
        part = slice(h * (tt // 2), (h + 1) * (tt // 2))
        lax.fori_loop(part.start // 4, part.stop // 4, second_rows, 0)
        writes.append(pltpu.make_async_copy(st.at[:, part], stepped.at[:, part], out_sem.at[h]))
        writes[h].start()

    lane3 = iota(coupled.shape, 2)
    inner = (
        jnp.where(lane3 == 0, 0.0, pltpu.roll(coupled, 1, 2))
        + jnp.where(lane3 == face_t - 1, 0.0, pltpu.roll(coupled, face_t - 1, 2))
        - 4.0 * coupled
    )
    arrive(edges, face_send, face_recv)
    lows = jnp.concatenate([hr[0, f : f + 1, :][None] for f in range(fields)], axis=0)
    highs = jnp.concatenate([hr[1, f : f + 1, :][None] for f in range(fields)], axis=0)
    down, up = shift_rows(coupled, lows, highs)
    put_low = jnp.where((row8 == 1) & (lane8 == 0), 1.0, 0.0)
    put_high = jnp.where((row8 == 0) & (lane8 == face_t - 1), 1.0, 0.0)
    both = jnp.concatenate([tr[0], tr[1]], axis=0)
    sides = lax.dot_general(
        both, jnp.concatenate([put_low, put_high], axis=0), (((0,), (0,)), ((), ())),
        precision=lax.Precision.HIGHEST, preferred_element_type=F32,
    ).reshape(coupled.shape)
    face[...] = coupled + 0.2 * (inner + (down + up) + sides)
    write_face = pltpu.make_async_copy(face, face_out, face_sem)
    write_face.start()

    leave(small, small_send, small_recv)
    leave(moves, halo_send, halo_recv)
    leave(edges, face_send, face_recv)
    all_dest.wait_send()
    all_vals.wait_send()
    for copy in writes:
        copy.wait()
    write_face.wait()


def body(corona, kappa, mixing, helio_prev, owner, dest_cell, corner_base, fractions):
    n_lat, n_lon = lax.axis_size("lat"), lax.axis_size("lon")
    n_dev = n_lat * n_lon
    fields, tt, pp, n_r = corona.shape
    count = corner_base.shape[0]
    face_p, face_t = helio_prev.shape[1:]
    ext = fields + 1
    hbm = pl.BlockSpec(memory_space=pltpu.HBM)
    free = pl.BlockSpec(memory_space=pl.ANY)
    sem = pltpu.SemaphoreType.DMA
    v = lambda *shape: pltpu.VMEM(shape, F32)
    return pl.pallas_call(
        functools.partial(kernel, n_lat, n_lon),
        out_shape=(
            jax.ShapeDtypeStruct(corona.shape, F32),
            jax.ShapeDtypeStruct(helio_prev.shape, F32),
        ),
        in_specs=[hbm] * 8,
        out_specs=(free, free),
        scratch_shapes=[
            pltpu.SMEM(mixing.shape, F32),
            v(*mixing.shape),
            v(fields, fields, 8, LANES),
            v(*helio_prev.shape),
            pltpu.VMEM((1, count), jnp.int32),
            pltpu.VMEM((1, count), jnp.int32),
            pltpu.VMEM((1, count), jnp.int32),
            v(3, count),
            v(*helio_prev.shape),
            v(tt + 4, fields, WIDE),
            v(tt + 4, 1, WIDE),
            v(tt + 2, fields, WIDE),
            v(tt + 2, fields, WIDE),
            v(7, tt + 2, 1, WIDE),
            v(ext, tt + 4, pp, n_r),
            v(4, ext, tt, n_r),
            v(ext, tt + 16, n_r),
            v(ext, tt + 16, n_r),
            v(2, ext, tt, n_r),
            v(4, 16, n_r),
            v(4, 16, n_r),
            v(fields, tt + 2, pp, n_r),
            v(fields, tt, n_r),
            v(fields, tt, n_r),
            v(fields, tt, pp, n_r),
            v(n_dev // GROUP, NPAR, GROUP, LANES),
            v(n_dev, 1, LANES),
            v(n_dev, 1, LANES),
            v(n_dev, fields, LANES),
            v(n_dev, fields, LANES),
            v(tt, fields, 2 * LANES),
            v(2, fields, face_t),
            v(2, fields, face_t),
            v(8, fields * face_p),
            v(2, 8, fields * face_p),
            v(fields * face_p, 2 * face_t),
            sem((9,)), sem((10,)), sem((10,)), sem((16,)), sem((16,)), sem((2,)), sem,
            sem, sem, sem, sem, sem((4,)), sem((4,)),
        ],
        compiler_params=pltpu.CompilerParams(
            collective_id=0, has_side_effects=True, vmem_limit_bytes=48 * 1024 * 1024
        ),
        name="corona_helio",
    )(
        *[
            pltpu.with_memory_space_constraint(x, pltpu.HBM)
            for x in (
                corona, kappa, mixing, helio_prev, owner.reshape(1, count), dest_cell.reshape(1, count),
                corner_base.reshape(1, count), fractions,
            )
        ]
    )


def solution(mesh):
    return jax.shard_map(
        body,
        mesh=mesh,
        in_specs=(
            P(None, "lat", "lon", None),
            P("lat", "lon", None),
            P(),
            P(None, "lon", "lat"),
            P(("lat", "lon"), None),
            P(("lat", "lon")),
            P(("lat", "lon")),
            P(None, ("lat", "lon")),
        ),
        out_specs=(P(None, "lat", "lon", None), P(None, "lon", "lat")),
        check_vma=False,
    )
```
